128 devices in a mesh: grp: 4 (over z), fsdp: 32 (over x, y, core).
Axes of the slice: x: 4, y: 4, z: 4, core: 2. Of those that a mesh axis runs over, the one named last changes fastest.
Arguments:
- tokens: bfloat16 [32768, 8192], P(('grp', 'fsdp')), may hold values from -6 to 6
- tenant: int32 [32768], P(('grp', 'fsdp')), may hold values from 0 to 511, as said below
- slot_table: int32 [4, 8], replicated, may hold values from 0 to 511, as said below
- weight: bfloat16 [8192, 1024], P('fsdp'), may hold values from -0.0625 to 0.0625
- adapter_a: bfloat16 [512, 524288], P('grp', 'fsdp'), may hold values from -0.0625 to 0.0625
- adapter_b: bfloat16 [512, 65536], P('grp', 'fsdp'), may hold values from -0.75 to 0.75
- cotangent: bfloat16 [32768, 1024], P(('grp', 'fsdp')), may hold values from -6 to 6
Outputs:
- output: bfloat16 [32768, 1024], P(('grp', 'fsdp'))
- token_grad: bfloat16 [32768, 8192], P(('grp', 'fsdp'))
- grad_a: bfloat16 [512, 524288], P('grp', 'fsdp')
- grad_b: bfloat16 [512, 65536], P('grp', 'fsdp')
The draws below stay inside these ranges and needn't reach their ends.
Inputs may be any that keep to these rules, and one draw needn't show every extreme that they name: `slot_table`: row g lists 8 distinct adapters; its entries k * 2 to k * 2 + 1 are adapters of owner block k, that is ids from k * 128 to (k + 1) * 128 - 1. `tenant`: each row's adapter is one listed in its group's row of slot_table, and every listed adapter is used by some row of that group.
All inputs are finite; a program needn't handle non-finite values.
Results may differ from the reference program's by a relative error of at most 0.019.
Values may be sent and summed in bfloat16 or wider, within the bound.
A program may use at most 128 MiB of HBM per device.

```python
import math
import jax
import jax.numpy as jnp
from jax import lax

D = 8192
V_WIDTH = 1024
RANK = 64
ADAPTERS = 512
CAP = 2
ROWS_DEV = 256
TOKENS = 32768
N_GRP = 4
N_FSDP = 32


def shift_first(order, target, wanted_row, row_index):
    place = jnp.argmax((order == target).astype(jnp.int32))
    rolled = jnp.roll(order, -place)
    return jnp.where(row_index == wanted_row, rolled, order)


def pick_tables(key):
    owned_count = ADAPTERS // N_GRP
    table_key = jax.random.fold_in(key, 11)
    split_keys = jax.random.split(table_key, N_GRP * N_GRP + 1)
    orders = jax.vmap(lambda single: jax.random.permutation(single, owned_count))(split_keys[1:])
    chosen = jax.random.randint(split_keys[0], (2,), 0, N_GRP)
    row_index = jnp.arange(N_GRP * N_GRP, dtype=jnp.int32)
    low_row = chosen[0] * N_GRP
    high_row = chosen[1] * N_GRP + N_GRP - 1
    orders = jax.vmap(shift_first, in_axes=(0, None, None, 0))(orders, 0, low_row, row_index)
    orders = jax.vmap(shift_first, in_axes=(0, None, None, 0))(orders, owned_count - 1, high_row, row_index)
    picked = orders[:, :CAP].reshape(N_GRP, N_GRP, CAP)
    offsets = (jnp.arange(N_GRP, dtype=jnp.int32) * owned_count)[None, :, None]
    return (picked + offsets).reshape(N_GRP, N_GRP * CAP).astype(jnp.int32)


def draw_slot_table(key, part):
    return pick_tables(key)


def draw_tenant(key, part):
    table = pick_tables(key)
    key = jax.random.fold_in(key, 5)
    slot_count = N_GRP * CAP
    group_rows = ROWS_DEV * N_FSDP
    first_key, second_key, third_key = jax.random.split(key, 3)
    raw = jax.random.randint(first_key, (N_GRP, group_rows), 0, slot_count * slot_count)
    skewed = raw * raw // (slot_count * slot_count * slot_count)
    offsets = jax.random.randint(second_key, (N_GRP, 1), 0, slot_count)
    slots = (skewed + offsets) % slot_count
    place_keys = jax.random.split(third_key, N_GRP)
    places = jax.vmap(lambda single: jax.random.permutation(single, group_rows)[:slot_count])(place_keys)
    every_slot = jnp.arange(slot_count, dtype=jnp.int32)
    slots = jax.vmap(lambda line, where_to: line.at[where_to].set(every_slot))(slots, places)
    chosen = jnp.take_along_axis(table, slots, axis=1)
    return chosen.reshape(-1).astype(jnp.int32)


def levels(stream_key, shape, cuts, smallest, high):
    gain, own = 1.0, jax.random.fold_in(stream_key, 6)
    for position, shards_of in cuts:
        draws = jnp.exp(jax.random.uniform(jax.random.fold_in(own, position), (shards_of,), jnp.float32, smallest / len(cuts), high / len(cuts)))
        gain = gain * jnp.repeat(draws, shape[position] // shards_of).reshape([-1 if axis == position else 1 for axis in range(len(shape))])
    return gain


def scatter_about(key, extent, width, limit, cuts=(), kind=jnp.bfloat16):
    array = jax.random.normal(key, extent, jnp.float32) * width
    if len(cuts) > 0:
        array = levels(key, extent, cuts, -0.22, 0.18) * array
    return jnp.clip(array, min=-limit, max=limit).astype(kind)


def setup_inputs(seed: int = 0) -> dict:
    streams_of = jax.random.split(jax.random.key(seed), 8)
    tokens = scatter_about(streams_of[0], (TOKENS, D), 1.0, 6.0, ((0, 128),))
    tenant = draw_tenant(jax.random.fold_in(streams_of[7], 71), 0)
    slot_table = draw_slot_table(jax.random.fold_in(streams_of[7], 71), 0)
    weight = scatter_about(streams_of[3], (D, V_WIDTH), D ** -0.5, 0.0625, ((0, 32),))
    adapter_a = scatter_about(streams_of[4], (ADAPTERS, RANK * D), D ** -0.5, 0.0625, ((0, 4), (1, 32)))
    adapter_b = scatter_about(streams_of[5], (ADAPTERS, RANK * V_WIDTH), RANK ** -0.5, 0.75, ((0, 4), (1, 32)))
    cotangent = scatter_about(streams_of[6], (TOKENS, V_WIDTH), 1.0, 6.0, ((0, 128),))
    return {"tokens": tokens, "tenant": tenant, "slot_table": slot_table, "weight": weight, "adapter_a": adapter_a, "adapter_b": adapter_b, "cotangent": cotangent}


SCALE = 2.0

def contract_last(left, right):
    return lax.dot_general(left, right, (((1,), (1,)), ((), ())), preferred_element_type=jnp.float32)

def contract_first(left, right):
    return lax.dot_general(left, right, (((0,), (0,)), ((), ())), preferred_element_type=jnp.float32)

def reference(tokens, tenant, slot_table, weight, adapter_a, adapter_b, cotangent):
    slot_count = N_GRP * CAP
    owned_count = ADAPTERS // N_GRP
    row_scale = 1.0 / math.sqrt(ROWS_DEV * N_FSDP)
    full_a = adapter_a.reshape(ADAPTERS, RANK, D)
    full_b = adapter_b.reshape(ADAPTERS, RANK, V_WIDTH)
    tok_grp = tokens.reshape(N_GRP, N_FSDP, ROWS_DEV, D)
    ten_grp = tenant.reshape(N_GRP, N_FSDP * ROWS_DEV)
    cot_grp = cotangent.reshape(N_GRP, N_FSDP, ROWS_DEV, V_WIDTH)

    def one_group(inputs):
        tok_dev, ten_rows, cot_dev, group_ids = inputs
        stack_a = jnp.take(full_a, group_ids, axis=0).reshape(slot_count * RANK, D)
        stack_b = jnp.take(full_b, group_ids, axis=0).reshape(slot_count * RANK, V_WIDTH)
        tok_all = tok_dev.reshape(-1, D)
        cot_all = cot_dev.reshape(-1, V_WIDTH)
        row_mask = jnp.repeat((ten_rows[:, None] == group_ids[None, :]).astype(jnp.float32), RANK, axis=1)
        low_proj = (contract_last(tok_all, stack_a) * row_mask).astype(jnp.bfloat16)
        base_out = jnp.dot(tok_all, weight, preferred_element_type=jnp.float32)
        output = (base_out + SCALE * jnp.dot(low_proj, stack_b, preferred_element_type=jnp.float32)).astype(jnp.bfloat16)
        back_proj = (SCALE * row_mask * contract_last(cot_all, stack_b)).astype(jnp.bfloat16)
        token_grad = (contract_last(cot_all, weight) + jnp.dot(back_proj, stack_a, preferred_element_type=jnp.float32)).astype(jnp.bfloat16)
        low_dev = low_proj.reshape(N_FSDP, ROWS_DEV, slot_count * RANK)
        back_dev = back_proj.reshape(N_FSDP, ROWS_DEV, slot_count * RANK)

        def add_device(carry, item):
            sum_a, sum_b = carry
            tok_one, cot_one, low_one, back_one = item
            term_a = lax.optimization_barrier((contract_first(back_one, tok_one) * row_scale).astype(jnp.bfloat16))
            term_b = lax.optimization_barrier((contract_first(low_one, cot_one) * (SCALE * row_scale)).astype(jnp.bfloat16))
            return ((sum_a + term_a.astype(jnp.float32), sum_b + term_b.astype(jnp.float32)), None)
        start = (jnp.zeros((slot_count * RANK, D), jnp.float32), jnp.zeros((slot_count * RANK, V_WIDTH), jnp.float32))
        (sum_a, sum_b), _ = lax.scan(add_device, start, (tok_dev, cot_dev, low_dev, back_dev))
        return (output, token_grad, sum_a.reshape(slot_count, RANK * D), sum_b.reshape(slot_count, RANK * V_WIDTH))
    outputs, token_grads, group_a, group_b = lax.map(one_group, (tok_grp, ten_grp, cot_grp, slot_table))
    flat_a = group_a.reshape(N_GRP * slot_count, RANK * D)
    flat_b = group_b.reshape(N_GRP * slot_count, RANK * V_WIDTH)
    flat_ids = slot_table.reshape(-1)

    def owner_block(first):
        owner_hits = ((first + jnp.arange(owned_count, dtype=jnp.int32))[:, None] == flat_ids[None, :]).astype(jnp.float32)
        block_a = jnp.dot(owner_hits, flat_a, precision=lax.Precision.HIGHEST, preferred_element_type=jnp.float32)
        block_b = jnp.dot(owner_hits, flat_b, precision=lax.Precision.HIGHEST, preferred_element_type=jnp.float32)
        return (block_a.astype(jnp.bfloat16), block_b.astype(jnp.bfloat16))
    firsts = jnp.arange(N_GRP, dtype=jnp.int32) * owned_count
    blocks_a, blocks_b = lax.map(owner_block, firsts)
    output = outputs.reshape(TOKENS, V_WIDTH)
    token_grad = token_grads.reshape(TOKENS, D)
    grad_a = blocks_a.reshape(ADAPTERS, RANK * D)
    grad_b = blocks_b.reshape(ADAPTERS, RANK * V_WIDTH)
    return (output, token_grad, grad_a, grad_b)
```

```python
import math

import jax
import jax.numpy as jnp
from jax import lax
from jax.sharding import PartitionSpec as P

SCALE = 2.0


def contract_last(left, right):
    return lax.dot_general(
        left, right, (((1,), (1,)), ((), ())), preferred_element_type=jnp.float32
    )


def contract_first(left, right):
    return lax.dot_general(
        left, right, (((0,), (0,)), ((), ())), preferred_element_type=jnp.float32
    )


def local(tokens, tenant, slot_table, weight, adapter_a, adapter_b, cotangent):
    row_count, width = tokens.shape
    out_width = weight.shape[1]
    group_count = lax.axis_size("grp")
    part_count = lax.axis_size("fsdp")
    group_id = lax.axis_index("grp")
    slot_count = slot_table.shape[1]
    per_owner = slot_count // group_count
    owned_count = adapter_a.shape[0]
    width_a = adapter_a.shape[1]
    width_b = adapter_b.shape[1]
    own_ranks = width_a // width
    own_slots = lax.dynamic_index_in_dim(slot_table, group_id, 0, keepdims=False)
    wanted = (
        lax.dynamic_slice_in_dim(slot_table, group_id * per_owner, per_owner, 1)
        - group_id * owned_count
    )
    hits = (
        wanted.reshape(-1, 1) == jnp.arange(owned_count, dtype=jnp.int32)[None, :]
    ).astype(jnp.bfloat16)
    chosen_b = jnp.dot(hits, adapter_b, preferred_element_type=jnp.float32).astype(jnp.bfloat16)
    chosen_a = jnp.dot(hits, adapter_a, preferred_element_type=jnp.float32).astype(jnp.bfloat16)

    def exchange(chosen):
        return lax.all_to_all(
            chosen.reshape(group_count, per_owner, -1), "grp", 0, 0, tiled=True
        )

    landed_b = exchange(chosen_b).reshape(slot_count * own_ranks, out_width)
    landed_a = exchange(chosen_a).reshape(slot_count * own_ranks, width)
    stack_b = lax.all_gather(landed_b, "fsdp", axis=0, tiled=True)
    stack_a = lax.all_gather(landed_a, "fsdp", axis=0, tiled=True)
    full_weight = lax.all_gather(weight, "fsdp", axis=0, tiled=True)
    row_mask = jnp.tile(
        jnp.repeat((tenant[:, None] == own_slots[None, :]).astype(jnp.float32), own_ranks, axis=1),
        (1, part_count),
    )
    row_scale = 1.0 / math.sqrt(row_count * part_count)
    back_proj = (SCALE * row_mask * contract_last(cotangent, stack_b)).astype(jnp.bfloat16)
    term_a = (contract_first(back_proj, tokens) * row_scale).astype(jnp.bfloat16)
    summed_a = lax.psum_scatter(term_a, "fsdp", scatter_dimension=0, tiled=True)
    low_proj = (contract_last(tokens, stack_a) * row_mask).astype(jnp.bfloat16)
    term_b = (contract_first(low_proj, cotangent) * (SCALE * row_scale)).astype(jnp.bfloat16)
    summed_b = lax.psum_scatter(term_b, "fsdp", scatter_dimension=0, tiled=True)
    base_out = jnp.dot(tokens, full_weight, preferred_element_type=jnp.float32)
    output = (
        base_out + SCALE * jnp.dot(low_proj, stack_b, preferred_element_type=jnp.float32)
    ).astype(jnp.bfloat16)
    token_grad = (
        contract_last(cotangent, full_weight)
        + jnp.dot(back_proj, stack_a, preferred_element_type=jnp.float32)
    ).astype(jnp.bfloat16)
    home_a = exchange(summed_a.reshape(slot_count, width_a)).reshape(slot_count, width_a)
    home_b = exchange(summed_b.reshape(slot_count, width_b)).reshape(slot_count, width_b)
    grad_a = contract_first(hits, home_a).astype(jnp.bfloat16)
    grad_b = contract_first(hits, home_b).astype(jnp.bfloat16)
    return (output, token_grad, grad_a, grad_b)


def solution(mesh):
    return jax.shard_map(
        local,
        mesh=mesh,
        in_specs=(
            P(("grp", "fsdp"), None),
            P(("grp", "fsdp")),
            P(),
            P("fsdp", None),
            P("grp", "fsdp"),
            P("grp", "fsdp"),
            P(("grp", "fsdp"), None),
        ),
        out_specs=(
            P(("grp", "fsdp"), None),
            P(("grp", "fsdp"), None),
            P("grp", "fsdp"),
            P("grp", "fsdp"),
        ),
        check_vma=False,
    )
```

```python
import math

import jax
import jax.numpy as jnp
from jax import lax
from jax.experimental import pallas as pl
from jax.experimental.pallas import tpu as pltpu
from jax.sharding import PartitionSpec as P

SCALE = 2.0
RING = 4
MESSAGES = 200
MESH = pl.DeviceIdType.MESH
ALL = slice(None)
BF16 = jnp.bfloat16
F32 = jnp.float32


def mod(value):
    return lax.rem(value + RING, RING)


def mm(left, right):
    return jnp.dot(left, right, preferred_element_type=F32)


def mm_last(left, right):
    return lax.dot_general(left, right, (((1,), (1,)), ((), ())), preferred_element_type=F32)


def mm_first(left, right):
    return lax.dot_general(left, right, (((0,), (0,)), ((), ())), preferred_element_type=F32)


class Net:
    def __init__(self, send_sems, recv_sems):
        self.z = lax.axis_index("grp")
        part = lax.axis_index("fsdp")
        self.c = lax.rem(part, 2)
        self.y = lax.rem(part // 2, RING)
        self.x = part // (2 * RING)
        self.send_sems, self.recv_sems, self.started = send_sems, recv_sems, []

    def at(self, dx=0, dy=0, dz=0, dc=0):
        x, y, z = mod(self.x + dx), mod(self.y + dy), mod(self.z + dz)
        c = lax.rem(self.c + dc, 2)
        return (z, (x * RING + y) * 2 + c)

    def plane(self, axis, step):
        return self.at(dx=step) if axis == 0 else self.at(dy=step)

    def send(self, source, target, device):
        k = len(self.started)
        copy = pltpu.make_async_remote_copy(
            src_ref=source,
            dst_ref=target,
            send_sem=self.send_sems.at[k],
            recv_sem=self.recv_sems.at[k],
            device_id=device,
            device_id_type=MESH,
        )
        copy.start()
        self.started.append(copy)
        return copy

    def sibling(self, ref):
        return self.send(ref, ref, self.at(dc=1))


class Gather:
    def __init__(self, net, ref, width, rows=ALL, to_sibling=True):
        self.net, self.buffer, self.quarter, self.rows = net, ref, width // 4, rows
        self.to_sibling = to_sibling
        self.near, self.far, self.line, self.rest, self.passed = {}, {}, {}, {}, []

    def ref(self, half, p, s, part, count):
        x, y = (p, s) if half == 0 else (s, p)
        cols = pl.ds((half * 2 + part) * self.quarter, count * self.quarter)
        return self.buffer.at[self.net.c, x, y, self.rows, cols]

    def place(self, half):
        return (self.net.x, self.net.y) if half == 0 else (self.net.y, self.net.x)

    def move(self, ref, axis, step):
        return self.net.send(ref, ref, self.net.plane(axis, step))

    def hand(self, ref):
        if self.to_sibling:
            self.passed.append(self.net.sibling(ref))

    def s1(self):
        for half in (0, 1):
            p, s = self.place(half)
            own = self.ref(half, p, s, 0, 2)
            self.near[half] = self.move(own, half, 1), self.move(own, half, -1)

    def s2(self):
        for half in (0, 1):
            p, s = self.place(half)
            plus, minus = self.near[half]
            plus.wait_recv()
            one = self.move(self.ref(half, mod(p - 1), s, 0, 1), half, 1)
            minus.wait_recv()
            two = self.move(self.ref(half, mod(p + 1), s, 1, 1), half, -1)
            self.far[half] = one, two

    def s3(self):
        for half in (0, 1):
            _, s = self.place(half)
            for copy in self.far[half]:
                copy.wait_recv()
            own = self.ref(half, ALL, s, 0, 2)
            self.line[half] = self.move(own, 1 - half, 1), self.move(own, 1 - half, -1)
            self.hand(own)

    def s4(self):
        for half in (0, 1):
            _, s = self.place(half)
            plus, minus = self.line[half]
            plus.wait_recv()
            one = self.move(self.ref(half, ALL, mod(s - 1), 0, 1), 1 - half, 1)
            minus.wait_recv()
            two = self.move(self.ref(half, ALL, mod(s + 1), 1, 1), 1 - half, -1)
            self.rest[half] = one, two
            self.hand(self.ref(half, ALL, mod(s - 1), 0, 2))
            self.hand(self.ref(half, ALL, mod(s + 1), 0, 2))

    def s5(self):
        for half in (0, 1):
            _, s = self.place(half)
            for copy in self.rest[half]:
                copy.wait_recv()
            self.hand(self.ref(half, ALL, mod(s + 2), 0, 2))

    def finish(self):
        for copy in self.passed:
            copy.wait_recv()


class Scatter:
    def __init__(self, net, terms, line_slots, block_slots, out, width):
        self.net, self.terms, self.out, self.quarter = net, terms, out, width // 4
        self.line_slots, self.block_slots = line_slots, block_slots
        self.copies = {}

    def index(self, half, p, s, part):
        x, y = (p, s) if half == 0 else (s, p)
        return x, y, ALL, pl.ds((half * 2 + part) * self.quarter, self.quarter)

    def place(self, half):
        return (self.net.x, self.net.y) if half == 0 else (self.net.y, self.net.x)

    def first(self, half, slots, axis, block):
        me = self.net.x if axis == 0 else self.net.y
        ahead, behind = self.net.plane(axis, 1), self.net.plane(axis, -1)
        at = self.terms.at
        self.copies[half] = [
            self.net.send(at[block(mod(me + 2), 0)], slots.at[half, 0], ahead),
            self.net.send(at[block(mod(me + 1), 1)], slots.at[half, 1], ahead),
            self.net.send(at[block(mod(me + 2), 1)], slots.at[half, 2], behind),
            self.net.send(at[block(mod(me - 1), 0)], slots.at[half, 3], behind),
        ]

    def add(self, block, slots):
        total = self.terms[block].astype(F32)
        for slot in slots:
            total = total + slot.astype(F32)
        return total

    def s1(self):
        for half in (0, 1):
            self.first(half, self.line_slots, half, lambda p, part, h=half: self.index(h, p, ALL, part))

    def s2(self):
        for half in (0, 1):
            p, _ = self.place(half)
            copies = self.copies[half]
            for k, step, part, slot in ((0, 1, 0, 4), (2, -1, 1, 5)):
                copies[k].wait_recv()
                target = mod(p + step)

                def line(i, _, half=half, k=k, part=part, target=target):
                    block = self.index(half, target, i, part)
                    self.terms[block] = self.add(block, [self.line_slots[half, k, i]]).astype(BF16)
                    return 0

                lax.fori_loop(0, RING, line, 0)
                copies.append(
                    self.net.send(
                        self.terms.at[self.index(half, target, ALL, part)],
                        self.line_slots.at[half, slot],
                        self.net.plane(half, step),
                    )
                )

    def s3(self):
        for half in (0, 1):
            p, _ = self.place(half)
            copies = self.copies[half]
            for k in (1, 3, 4, 5):
                copies[k].wait_recv()
            for part, one, two in ((0, 4, 3), (1, 5, 1)):

                def line(i, _, half=half, part=part, one=one, two=two, p=p):
                    block = self.index(half, p, i, part)
                    slots = [self.line_slots[half, one, i], self.line_slots[half, two, i]]
                    self.terms[block] = self.add(block, slots).astype(BF16)
                    return 0

                lax.fori_loop(0, RING, line, 0)
            self.first(
                half, self.block_slots, 1 - half, lambda s, part, h=half, p=p: self.index(h, p, s, part)
            )

    def s4(self):
        for half in (0, 1):
            p, s = self.place(half)
            copies = self.copies[half]
            for k, step, part, slot in ((0, 1, 0, 4), (2, -1, 1, 5)):
                copies[k].wait_recv()
                block = self.index(half, p, mod(s + step), part)
                self.terms[block] = self.add(block, [self.block_slots[half, k]]).astype(BF16)
                copies.append(
                    self.net.send(
                        self.terms.at[block],
                        self.block_slots.at[half, slot],
                        self.net.plane(1 - half, step),
                    )
                )

    def s5(self):
        for half in (0, 1):
            p, s = self.place(half)
            for k in (1, 3, 4, 5):
                self.copies[half][k].wait_recv()
            for part, one, two in ((0, 4, 3), (1, 5, 1)):
                block = self.index(half, p, s, part)
                slots = [self.block_slots[half, one], self.block_slots[half, two]]
                cols = pl.ds((half * 2 + part) * self.quarter, self.quarter)
                self.out[:, cols] = self.add(block, slots).astype(BF16)


def swap(net, source, landed):
    copies = [
        net.send(source.at[mod(net.z + step)], landed.at[net.z], net.at(dz=step)) for step in (1, 3, 2)
    ]
    landed[net.z] = source[net.z]
    return copies


def fold(q, shape, row_dim):
    row = lax.broadcasted_iota(jnp.int32, shape, row_dim)
    col = lax.broadcasted_iota(jnp.int32, shape, 1 - row_dim)
    same = (row // 4 == col // 16) & (row % 4 == col % 4) & ((col // 4) % 4 == q)
    return jnp.where(same, 1.0, 0.0).astype(BF16)


def kernel(
    picks, mask, tokens, weight, adapter_a, adapter_b, cotangent,
    output, token_grad, home_a, home_b,
    w, sa, sb, tok, cot, tg, ab, t_a, t_b, lx_a, ly_a, lx_b, ly_b, g_a, g_b,
    back, low, back_t, low_t, back_x, low_x, total, pa, pb, ma, mb, ha, hb, na, nb,
    local_sems, send_sems, recv_sems,
):
    net = Net(send_sems, recv_sems)
    x, y, z, c = net.x, net.y, net.z, net.c
    width, out_width = tokens.shape[1], weight.shape[1]
    rows = tokens.shape[0]
    part = width // 4
    part_b = out_width // 4
    row_scale = 1.0 / math.sqrt(rows * 2 * RING * RING)

    loads = [
        pltpu.make_async_copy(adapter_b, ab, local_sems.at[0]),
        pltpu.make_async_copy(weight, w.at[c, x, y], local_sems.at[1]),
        pltpu.make_async_copy(adapter_a.at[:, pl.ds(0, width)], tg.at[pl.ds(0, 128)], local_sems.at[2]),
        pltpu.make_async_copy(adapter_a.at[:, pl.ds(width, width)], tg.at[pl.ds(128, 128)], local_sems.at[3]),
        pltpu.make_async_copy(cotangent, cot.at[c], local_sems.at[4]),
        pltpu.make_async_copy(tokens, tok.at[c], local_sems.at[5]),
    ]
    for load in loads:
        load.start()

    barrier = pltpu.get_barrier_semaphore()
    partners = [net.at(dx=1), net.at(dx=-1), net.at(dy=1), net.at(dy=-1), net.at(dz=1), net.at(dz=-1)]
    partners += [net.at(dz=2), net.at(dc=1)]
    for device in partners:
        pl.semaphore_signal(barrier, inc=1, device_id=device, device_id_type=MESH)
    pl.semaphore_wait(barrier, len(partners))

    own_rows = pl.ds(pl.multiple_of(z * 64, 64), 64)
    gather_w = Gather(net, w, out_width, rows=own_rows, to_sibling=False)
    gather_a = Gather(net, sa, width)
    gather_b = Gather(net, sb, out_width)
    scatter_a = Scatter(net, t_a, lx_a, ly_a, g_a, width)
    scatter_b = Scatter(net, t_b, lx_b, ly_b, g_b, out_width)

    loads[1].wait()
    gather_w.s1()

    loads[0].wait()
    chosen = jnp.zeros((64, part_b), F32)
    for i in range(8):
        chosen += mm(picks[i], ab[:, i * part_b : (i + 1) * part_b])
    pb[...] = chosen.astype(BF16).reshape(pb.shape)
    land_b = swap(net, pb, mb)
    loads[2].wait()
    loads[3].wait()

    def pick_a(k, _):
        cols = pl.ds(pl.multiple_of(k * 512, 512), 512)
        chosen = jnp.zeros((64, 512), F32)
        for i in range(8):
            r, q = i // 4, i % 4
            from_cols = pl.ds(pl.multiple_of(q * part + k * 512, 512), 512)
            chosen += mm(picks[i], tg[r * 128 : (r + 1) * 128, from_cols])
        pa[:, :, cols] = chosen.astype(BF16).reshape(4, 16, 512)
        return 0

    lax.fori_loop(0, part // 512, pick_a, 0)
    land_a = swap(net, pa, ma)

    loads[4].wait()
    loads[5].wait()
    cot_x = net.sibling(cot.at[c])
    tok_x = net.sibling(tok.at[c])

    for copy in land_b:
        copy.wait_recv()
    landed = mb[...].reshape(64, part_b)
    for q in range(4):
        sb[c, x, y, :, q * part_b : (q + 1) * part_b] = mm(fold(q, (16, 64), 0), landed).astype(BF16)
    gather_b.s1()
    gather_w.s2()
    for copy in land_a:
        copy.wait_recv()
    landed = ma[...].reshape(64, part)
    for q in range(4):
        sa[c, x, y, :, q * part : (q + 1) * part] = mm(fold(q, (16, 64), 0), landed).astype(BF16)
    gather_b.s2()
    gather_a.s1()
    gather_b.s3()
    gather_w.s3()
    gather_b.s4()
    gather_a.s2()
    gather_w.s4()
    gather_b.s5()
    gather_w.s5()

    quarter = lambda k, dz, cols=ALL: w.at[
        c, k, :, pl.ds(pl.multiple_of(mod(z + dz) * 64, 64), 64), cols
    ]
    ring, ring_far, passed = {}, {}, {}

    def z_start(k):
        own = quarter(k, 0)
        ring[k] = net.send(own, own, net.at(dz=1)), net.send(own, own, net.at(dz=-1))
        passed[k] = [net.sibling(own)]

    def z_forward(k):
        half = out_width // 2
        plus, minus = ring[k]
        plus.wait_recv()
        one = quarter(k, -1, pl.ds(0, half))
        one = net.send(one, one, net.at(dz=1))
        minus.wait_recv()
        two = quarter(k, 1, pl.ds(half, half))
        two = net.send(two, two, net.at(dz=-1))
        ring_far[k] = one, two
        passed[k] += [net.sibling(quarter(k, -1)), net.sibling(quarter(k, 1))]
        if k + 2 < RING:
            z_start(k + 2)

    def z_finish(k):
        for copy in ring_far[k]:
            copy.wait_recv()
        passed[k].append(net.sibling(quarter(k, 2)))

    z_start(0)
    z_start(1)
    gather_a.s3()
    gather_b.finish()

    stack_b = lambda: sb[...].reshape(512, out_width)
    weights = mask[...].astype(F32)
    found = SCALE * weights * mm_last(cot[c], stack_b())
    back[...] = found.astype(BF16)
    back_t[...] = found.T.astype(BF16).reshape(2, 256, rows)
    swap_back = net.send(back_t.at[1 - c], back_x, net.at(dc=1))
    tok_x.wait_recv()
    cot_x.wait_recv()
    swap_back.wait_recv()

    def terms_a(k, _):
        cols = pl.ds(pl.multiple_of(k * 512, 512), 512)
        found = mm(back_t[c], tok[c, :, cols]) + mm(back_x[...], tok[1 - c, :, cols])
        t_a[:, :, :, cols] = (found * row_scale).astype(BF16).reshape(4, 4, 16, 512)
        return 0

    lax.fori_loop(0, width // 512, terms_a, 0)
    scatter_a.s1()
    gather_a.s4()
    z_forward(0)
    scatter_a.s2()
    gather_a.s5()
    gather_a.finish()

    def low_step(k, acc):
        cols = pl.ds(pl.multiple_of(k * 1024, 1024), 1024)
        return acc + mm_last(tok[c, :, cols], sa[:, :, :, :, cols].reshape(512, 1024))

    found = weights * lax.fori_loop(0, width // 1024, low_step, jnp.zeros((rows, 512), F32))
    low[...] = found.astype(BF16)
    low_t[...] = found.T.astype(BF16).reshape(2, 256, rows)
    swap_low = net.send(low_t.at[1 - c], low_x, net.at(dc=1))
    total[...] = SCALE * mm(low[...], stack_b())
    swap_low.wait_recv()
    found = mm(low_t[c], cot[c]) + mm(low_x[...], cot[1 - c])
    t_b[...] = (found * (SCALE * row_scale)).astype(BF16).reshape(4, 4, 16, out_width)
    scatter_b.s1()
    z_forward(1)
    scatter_a.s3()
    scatter_b.s2()
    scatter_b.s3()
    scatter_a.s4()
    scatter_b.s4()
    z_forward(2)

    stores = []

    def compute(k):
        z_finish(k)
        for copy in passed[k]:
            copy.wait_recv()

        def step(j, _):
            start = pl.multiple_of((k * RING + j) * 512, 512)
            one, two = w[0, k, j], w[1, k, j]
            cols, lo, hi = pl.ds(start, 512), pl.ds(start, 256), pl.ds(start + 256, 256)
            total[...] += mm(tok[c, :, lo], one) + mm(tok[c, :, hi], two)
            from_a = mm(back[...], sa[:, :, :, :, cols].reshape(512, 512))
            tg[:, lo] = (mm_last(cot[c], one) + from_a[:, :256]).astype(BF16)
            tg[:, hi] = (mm_last(cot[c], two) + from_a[:, 256:]).astype(BF16)
            return 0

        lax.fori_loop(0, RING, step, 0)
        cols = pl.ds(k * 4 * 512, 4 * 512)
        store = pltpu.make_async_copy(tg.at[:, cols], token_grad.at[:, cols], local_sems.at[6 + k])
        store.start()
        stores.append(store)

    compute(0)
    scatter_a.s5()
    scatter_b.s5()

    def unfold(source, target, size):
        found = jnp.zeros((64, size), F32)
        for q in range(4):
            found += mm(fold(q, (64, 16), 1), source[:, q * size : (q + 1) * size])
        target[...] = found.astype(BF16).reshape(4, 16, size)

    unfold(g_a, na, part)
    unfold(g_b, nb, part_b)
    back_a = swap(net, na, ha)
    back_b = swap(net, nb, hb)
    z_forward(3)
    compute(1)
    compute(2)
    for copy in back_a + back_b:
        copy.wait_recv()
    home_a[...] = ha[...].reshape(64, part)
    home_b[...] = hb[...].reshape(64, part_b)
    compute(3)
    output[...] = total[...].astype(BF16)
    for store in stores:
        store.wait()
    for copy in net.started:
        copy.wait_send()


def expand_kernel(picks, home_a, home_b, grad_a, grad_b):
    grad_a[...] = mm(picks[0], home_a[...]).astype(BF16)
    grad_b[...] = mm(picks[0], home_b[...]).astype(BF16)


def local(tokens, tenant, slot_table, weight, adapter_a, adapter_b, cotangent):
    rows, width = tokens.shape
    out_width = weight.shape[1]
    groups = lax.axis_size("grp")
    group = lax.axis_index("grp")
    slots = slot_table.shape[1]
    per_owner = slots // groups
    owned = adapter_a.shape[0]
    own_slots = lax.dynamic_index_in_dim(slot_table, group, 0, keepdims=False)
    wanted = lax.dynamic_slice_in_dim(slot_table, group * per_owner, per_owner, 1) - group * owned
    row = jnp.arange(64, dtype=jnp.int32)
    own_id = jnp.repeat(jnp.repeat(wanted, 2, axis=1), 4, axis=0).reshape(64)
    place = (row % 2) * 4 + (row // 4) % 4
    step = jnp.arange(8, dtype=jnp.int32)
    ids = jnp.arange(owned, dtype=jnp.int32)
    picks = (
        (own_id[None, :, None] == ids[None, None, :]) & (place[None, :, None] == step[:, None, None])
    ).astype(BF16)
    picks_t = (
        (own_id[None, None, :] == ids[None, :, None]) & (place[None, None, :] == step[:, None, None])
    ).astype(BF16)
    mask = jnp.tile(jnp.repeat(tenant[:, None] == own_slots[None, :], 2, axis=1), (1, 32)).astype(BF16)

    part, part_b = width // 4, out_width // 4
    vmem, hbm = pl.BlockSpec(memory_space=pltpu.VMEM), pl.BlockSpec(memory_space=pl.ANY)
    buffer = lambda *shape, dtype=BF16: pltpu.VMEM(shape, dtype)
    output, token_grad, home_a, home_b = pl.pallas_call(
        kernel,
        name="exchange_and_multiply",
        out_shape=(
            jax.ShapeDtypeStruct((rows, out_width), BF16),
            jax.ShapeDtypeStruct((rows, width), BF16),
            jax.ShapeDtypeStruct((64, part), BF16),
            jax.ShapeDtypeStruct((64, part_b), BF16),
        ),
        in_specs=[vmem, vmem, hbm, hbm, hbm, hbm, hbm],
        out_specs=(vmem, hbm, vmem, vmem),
        scratch_shapes=[
            buffer(2, 4, 4, 256, out_width),
            buffer(2, 4, 4, 16, width),
            buffer(2, 4, 4, 16, out_width),
            buffer(2, rows, width),
            buffer(2, rows, out_width),
            buffer(rows, width),
            buffer(owned, 2 * out_width),
            buffer(4, 4, 16, width),
            buffer(4, 4, 16, out_width),
            buffer(2, 6, 4, 16, part),
            buffer(2, 6, 16, part),
            buffer(2, 6, 4, 16, part_b),
            buffer(2, 6, 16, part_b),
            buffer(16, width),
            buffer(16, out_width),
            buffer(rows, 512),
            buffer(rows, 512),
            buffer(2, 256, rows),
            buffer(2, 256, rows),
            buffer(256, rows),
            buffer(256, rows),
            buffer(rows, out_width, dtype=F32),
            buffer(4, 16, part),
            buffer(4, 16, part_b),
            buffer(4, 16, part),
            buffer(4, 16, part_b),
            buffer(4, 16, part),
            buffer(4, 16, part_b),
            buffer(4, 16, part),
            buffer(4, 16, part_b),
            pltpu.SemaphoreType.DMA((10,)),
            pltpu.SemaphoreType.DMA((MESSAGES,)),
            pltpu.SemaphoreType.DMA((MESSAGES,)),
        ],
        compiler_params=pltpu.CompilerParams(
            collective_id=0, has_side_effects=True, vmem_limit_bytes=62 * 1024 * 1024
        ),
    )(picks, mask, tokens, weight, adapter_a, adapter_b, cotangent)

    grad_a, grad_b = pl.pallas_call(
        expand_kernel,
        name="expand_grads",
        grid=(8,),
        out_shape=(
            jax.ShapeDtypeStruct(adapter_a.shape, BF16),
            jax.ShapeDtypeStruct(adapter_b.shape, BF16),
        ),
        in_specs=[
            pl.BlockSpec((1, owned, 64), lambda i: (i, 0, 0)),
            pl.BlockSpec((64, part), lambda i: (0, 0)),
            pl.BlockSpec((64, part_b), lambda i: (0, 0)),
        ],
        out_specs=(
            pl.BlockSpec((owned, part), lambda i: (0, i)),
            pl.BlockSpec((owned, part_b), lambda i: (0, i)),
        ),
    )(picks_t, home_a, home_b)
    return (output, token_grad, grad_a, grad_b)


def solution(mesh):
    return jax.shard_map(
        local,
        mesh=mesh,
        in_specs=(
            P(("grp", "fsdp"), None),
            P(("grp", "fsdp")),
            P(),
            P("fsdp", None),
            P("grp", "fsdp"),
            P("grp", "fsdp"),
            P(("grp", "fsdp"), None),
        ),
        out_specs=(
            P(("grp", "fsdp"), None),
            P(("grp", "fsdp"), None),
            P("grp", "fsdp"),
            P("grp", "fsdp"),
        ),
        check_vma=False,
    )
```

```python
import math

import jax
import jax.numpy as jnp
from jax import lax
from jax.experimental import pallas as pl
from jax.experimental.pallas import tpu as pltpu
from jax.sharding import PartitionSpec as P

SCALE = 2.0
RING = 4
SENDS = 64
RECEIVES = 120
ORDER = (
    "w.s1", "d.s1", "swapb", "b.s1", "w.s2", "swapa", "tokx", "d.s2", "b.s2", "w.s3", "a.s1", "b.s3",
    "w.s4", "a.s2", "d.s3", "w.s5", "z0.go", "b.s4", "z1.go", "z2.go", "a.s3", "b.s5", "z0.fw", "d.s4",
    "b.fin", "back", "a.s4", "T0", "T1", "T2", "r0.s1", "z1.fw", "a.s5", "T3", "r1.s1", "a.fin", "d.s5",
    "low0", "z2.fw", "low1", "r0.s2", "z0.en", "z3.go", "tot", "tb", "d.fin", "q.s1", "r1.s2", "z1.en",
    "m0.0", "m1.0", "z4.go", "z2.en", "m0.1", "q.s2", "r0.s3", "m2.0", "r1.s3", "z3.fw", "q.s3", "r0.s4",
    "m1.1", "r1.s4", "q.s4", "z4.fw", "m2.1", "r0.s5", "z3.en", "r1.s5", "q.s5", "unf", "home", "m3.0",
    "z4.en", "m3.1", "m4.0", "m4.1", "homw", "out",
)
SHARED = 64
MESH = pl.DeviceIdType.MESH
ALL = slice(None)
BF16 = jnp.bfloat16
F32 = jnp.float32


def mod(value):
    return lax.rem(value + RING, RING)


def mm(left, right):
    return jnp.dot(left, right, preferred_element_type=F32)


def mm_last(left, right):
    return lax.dot_general(left, right, (((1,), (1,)), ((), ())), preferred_element_type=F32)


def mm_first(left, right):
    return lax.dot_general(left, right, (((0,), (0,)), ((), ())), preferred_element_type=F32)


class Net:
    def __init__(self, send_sems, recv_sems):
        self.z = lax.axis_index("grp")
        part = lax.axis_index("fsdp")
        self.c = lax.rem(part, 2)
        self.y = lax.rem(part // 2, RING)
        self.x = part // (2 * RING)
        self.send_sems, self.recv_sems, self.started, self.places = send_sems, recv_sems, [], 0

    def at(self, dx=0, dy=0, dz=0, dc=0):
        x, y, z = mod(self.x + dx), mod(self.y + dy), mod(self.z + dz)
        c = lax.rem(self.c + dc, 2)
        return (z, (x * RING + y) * 2 + c)

    def plane(self, axis, step):
        return self.at(dx=step) if axis == 0 else self.at(dy=step)

    def place(self):
        self.places += 1
        return self.recv_sems.at[self.places - 1]

    def send(self, source, target, device, sem=None):
        k = len(self.started)
        if k >= SENDS:
            self.started[k - SENDS].wait_send()
        copy = pltpu.make_async_remote_copy(
            src_ref=source,
            dst_ref=target,
            send_sem=self.send_sems.at[k % SENDS],
            recv_sem=self.place() if sem is None else sem,
            device_id=device,
            device_id_type=MESH,
        )
        copy.start()
        self.started.append(copy)
        return copy

    def sibling(self, ref, sem=None):
        return self.send(ref, ref, self.at(dc=1), sem)


def wait_all(region, sem):
    pltpu.make_async_copy(region, region, sem).wait()


class Gather:
    def __init__(self, net, ref, width, rows=ALL, to_sibling=True):
        self.net, self.buffer, self.quarter, self.rows = net, ref, width // 4, rows
        self.near, self.line = {}, {}
        self.far = [net.place(), net.place()]
        self.rest = [net.place(), net.place()]
        self.passed = net.place() if to_sibling else None

    def ref(self, half, p, s, part, count):
        x, y = (p, s) if half == 0 else (s, p)
        cols = pl.ds((half * 2 + part) * self.quarter, count * self.quarter)
        return self.buffer.at[self.net.c, x, y, self.rows, cols]

    def at(self, half):
        return (self.net.x, self.net.y) if half == 0 else (self.net.y, self.net.x)

    def move(self, ref, axis, step, sem=None):
        return self.net.send(ref, ref, self.net.plane(axis, step), sem)

    def hand(self, ref):
        if self.passed is not None:
            self.net.sibling(ref, self.passed)

    def s1(self):
        for half in (0, 1):
            p, s = self.at(half)
            own = self.ref(half, p, s, 0, 2)
            self.near[half] = self.move(own, half, 1), self.move(own, half, -1)

    def s2(self):
        for half in (0, 1):
            p, s = self.at(half)
            plus, minus = self.near[half]
            plus.wait_recv()
            self.move(self.ref(half, mod(p - 1), s, 0, 1), half, 1, self.far[half])
            minus.wait_recv()
            self.move(self.ref(half, mod(p + 1), s, 1, 1), half, -1, self.far[half])

    def s3(self):
        for half in (0, 1):
            p, s = self.at(half)
            wait_all(self.ref(half, mod(p + 2), s, 0, 2), self.far[half])
            own = self.ref(half, ALL, s, 0, 2)
            self.line[half] = self.move(own, 1 - half, 1), self.move(own, 1 - half, -1)
            self.hand(own)

    def s4(self):
        for half in (0, 1):
            _, s = self.at(half)
            plus, minus = self.line[half]
            plus.wait_recv()
            self.move(self.ref(half, ALL, mod(s - 1), 0, 1), 1 - half, 1, self.rest[half])
            minus.wait_recv()
            self.move(self.ref(half, ALL, mod(s + 1), 1, 1), 1 - half, -1, self.rest[half])
            self.hand(self.ref(half, ALL, mod(s - 1), 0, 2))
            self.hand(self.ref(half, ALL, mod(s + 1), 0, 2))

    def s5(self):
        for half in (0, 1):
            _, s = self.at(half)
            last = self.ref(half, ALL, mod(s + 2), 0, 2)
            wait_all(last, self.rest[half])
            self.hand(last)

    def fin(self):
        wait_all(self.buffer.at[1 - self.net.c, :, :, self.rows], self.passed)


class Scatter:
    def __init__(self, net, terms, line_slots, block_slots, out, width, base=0):
        self.net, self.terms, self.out, self.quarter, self.base = net, terms, out, width // 4, base
        self.line_slots, self.block_slots = line_slots, block_slots
        self.sems = [[[net.place() for _ in range(3)] for _ in range(2)] for _ in range(2)]

    def cols(self, half, part):
        return pl.ds(self.base + (half * 2 + part) * self.quarter, self.quarter)

    def index(self, half, p, s, part):
        x, y = (p, s) if half == 0 else (s, p)
        return x, y, ALL, self.cols(half, part)

    def at(self, half):
        return (self.net.x, self.net.y) if half == 0 else (self.net.y, self.net.x)

    def first(self, half, slots, axis, block, sems):
        me = self.net.x if axis == 0 else self.net.y
        ahead, behind = self.net.plane(axis, 1), self.net.plane(axis, -1)
        at, slots, net = self.terms.at, slots.at, self.net
        net.send(at[block(mod(me + 2), 0)], slots[half, 0], ahead, sems[0])
        net.send(at[block(mod(me + 2), 1)], slots[half, 1], behind, sems[1])
        net.send(at[block(mod(me + 1), 1)], slots[half, 2], ahead, sems[2])
        net.send(at[block(mod(me - 1), 0)], slots[half, 3], behind, sems[2])

    def add(self, block, slots):
        total = self.terms[block].astype(F32)
        for slot in slots:
            total = total + slot.astype(F32)
        return total

    def s1(self):
        for half in (0, 1):
            self.first(
                half,
                self.line_slots,
                half,
                lambda p, part, h=half: self.index(h, p, ALL, part),
                self.sems[0][half],
            )

    def s2(self):
        for half in (0, 1):
            p, _ = self.at(half)
            sems = self.sems[0][half]
            for k, step in ((0, 1), (1, -1)):
                wait_all(self.line_slots.at[half, k], sems[k])
                target = mod(p + step)

                def line(i, _, half=half, k=k, target=target):
                    block = self.index(half, target, i, k)
                    self.terms[block] = self.add(block, [self.line_slots[half, k, i]]).astype(BF16)
                    return 0

                lax.fori_loop(0, RING, line, 0)
                self.net.send(
                    self.terms.at[self.index(half, target, ALL, k)],
                    self.line_slots.at[half, 4 + k],
                    self.net.plane(half, step),
                    sems[2],
                )

    def s3(self):
        for half in (0, 1):
            p, _ = self.at(half)
            wait_all(self.line_slots.at[half, pl.ds(2, 4)], self.sems[0][half][2])
            for part in (0, 1):

                def line(i, _, half=half, part=part, p=p):
                    block = self.index(half, p, i, part)
                    slots = [self.line_slots[half, 4 + part, i], self.line_slots[half, 3 - part, i]]
                    self.terms[block] = self.add(block, slots).astype(BF16)
                    return 0

                lax.fori_loop(0, RING, line, 0)
            self.first(
                half,
                self.block_slots,
                1 - half,
                lambda s, part, h=half, p=p: self.index(h, p, s, part),
                self.sems[1][half],
            )

    def s4(self):
        for half in (0, 1):
            p, s = self.at(half)
            sems = self.sems[1][half]
            for k, step in ((0, 1), (1, -1)):
                wait_all(self.block_slots.at[half, k], sems[k])
                block = self.index(half, p, mod(s + step), k)
                self.terms[block] = self.add(block, [self.block_slots[half, k]]).astype(BF16)
                self.net.send(
                    self.terms.at[block],
                    self.block_slots.at[half, 4 + k],
                    self.net.plane(1 - half, step),
                    sems[2],
                )

    def s5(self):
        for half in (0, 1):
            p, s = self.at(half)
            wait_all(self.block_slots.at[half, pl.ds(2, 4)], self.sems[1][half][2])
            for part in (0, 1):
                block = self.index(half, p, s, part)
                slots = [self.block_slots[half, 4 + part], self.block_slots[half, 3 - part]]
                self.out[:, self.cols(half, part)] = self.add(block, slots).astype(BF16)


def swap(net, source, landed):
    sem = net.place()
    for step in (1, 3, 2):
        net.send(source.at[mod(net.z + step)], landed.at[net.z], net.at(dz=step), sem)
    landed[net.z] = source[net.z]
    return landed.at[pl.ds(0, 3)], sem


def fold(q, shape, row_dim):
    row = lax.broadcasted_iota(jnp.int32, shape, row_dim)
    col = lax.broadcasted_iota(jnp.int32, shape, 1 - row_dim)
    same = (row // 4 == col // 16) & (row % 4 == col % 4) & ((col // 4) % 4 == q)
    return jnp.where(same, 1.0, 0.0).astype(BF16)


def wanted(slot_table, z, owned, row):
    found = jnp.zeros(row.shape, jnp.int32)
    for g in range(4):
        for j in range(2):
            here = (row // 16 == g) & ((row // 2) % 2 == j)
            found = found + jnp.where(here, slot_table[g, 2 * z + j] - z * owned, 0)
    return found


def pick(ids, row, adapter, i):
    here = (ids == adapter) & ((row % 2) * 4 + (row // 4) % 4 == i)
    return jnp.where(here, 1.0, 0.0).astype(BF16)


def kernel(
    slot_table, tenant, tokens, weight, adapter_a, adapter_b, cotangent,
    output, token_grad, home_a, home_b,
    w, sa, sb, tok, cot, tg, ab, t_a, t_b, lx_0, ly_0, lx_1, ly_1, lx_b, ly_b, g_a, g_b,
    mask, back, low, back_t, low_t, back_x, low_x, total, pa, pb, ma, mb, ha, hb, na, nb,
    local_sems, send_sems, recv_sems,
):
    net = Net(send_sems, recv_sems)
    x, y, z, c = net.x, net.y, net.z, net.c
    width, out_width = tokens.shape[1], weight.shape[1]
    rows = tokens.shape[0]
    owned = adapter_a.shape[0]
    part = width // 4
    part_b = out_width // 4
    row_scale = 1.0 / math.sqrt(rows * 2 * RING * RING)
    shared, slab = pl.ds(0, SHARED), (256 - SHARED) // RING
    rows_of = lambda dz: pl.ds(pl.multiple_of(SHARED + mod(z + dz) * slab, 16), slab)

    loads = [
        pltpu.make_async_copy(weight.at[rows_of(0)], w.at[c, x, y, rows_of(0)], local_sems.at[0]),
        pltpu.make_async_copy(adapter_b, ab, local_sems.at[1]),
        pltpu.make_async_copy(weight.at[shared], w.at[c, x, y, shared], local_sems.at[2]),
        pltpu.make_async_copy(adapter_a.at[:, pl.ds(0, width)], tg.at[pl.ds(0, 128)], local_sems.at[3]),
        pltpu.make_async_copy(adapter_a.at[:, pl.ds(width, width)], tg.at[pl.ds(128, 128)], local_sems.at[4]),
        pltpu.make_async_copy(cotangent, cot.at[c], local_sems.at[5]),
        pltpu.make_async_copy(tokens, tok.at[c], local_sems.at[6]),
    ]
    for load in loads:
        load.start()

    barrier = pltpu.get_barrier_semaphore()
    partners = [net.at(dx=1), net.at(dx=-1), net.at(dy=1), net.at(dy=-1), net.at(dz=1), net.at(dz=-1)]
    partners += [net.at(dz=2), net.at(dc=1)]
    for device in partners:
        pl.semaphore_signal(barrier, inc=1, device_id=device, device_id_type=MESH)

    steps, state = {}, {}

    def step(name):
        def keep(function):
            steps[name] = function
            return function

        return keep

    def stages(name, collective):
        for stage in ("s1", "s2", "s3", "s4", "s5", "fin"):
            if hasattr(collective, stage):
                steps[name + "." + stage] = getattr(collective, stage)

    gather_w = Gather(net, w, out_width, rows=rows_of(0), to_sibling=False)
    gather_d = Gather(net, w, out_width, rows=shared)
    gather_a = Gather(net, sa, width)
    gather_b = Gather(net, sb, out_width)
    stages("w", gather_w)
    stages("d", gather_d)
    stages("a", gather_a)
    stages("b", gather_b)
    half = width // 2
    stages("r0", Scatter(net, t_a, lx_0, ly_0, g_a, half))
    stages("r1", Scatter(net, t_a, lx_1, ly_1, g_a, half, base=half))
    stages("q", Scatter(net, t_b, lx_b, ly_b, g_b, out_width))

    row = lax.broadcasted_iota(jnp.int32, (64, owned), 0)
    adapter = lax.broadcasted_iota(jnp.int32, (64, owned), 1)
    ids = wanted(slot_table, z, owned, row)
    picks = [pick(ids, row, adapter, i) for i in range(8)]
    slot = lax.broadcasted_iota(jnp.int32, (16, rows), 0) // 2
    slot_ids = jnp.zeros((16, rows), jnp.int32)
    for s in range(8):
        slot_ids = slot_ids + jnp.where(slot == s, slot_table[z, s], 0)
    hit = jnp.where(slot_ids == tenant[...], 1.0, 0.0)
    mask[...] = jnp.concatenate([hit] * 32, axis=0).T
    for load in loads[:3]:
        load.wait()
    chosen = jnp.zeros((64, part_b), F32)
    for i in range(8):
        chosen += mm(picks[i], ab[:, i * part_b : (i + 1) * part_b])
    pb[...] = chosen.astype(BF16).reshape(pb.shape)

    @step("swapb")
    def _():
        state["lb"] = swap(net, pb, mb)

    @step("swapa")
    def _():
        loads[3].wait()
        loads[4].wait()

        def pick_a(k, _):
            cols = pl.ds(pl.multiple_of(k * 512, 512), 512)
            chosen = jnp.zeros((64, 512), F32)
            for i in range(8):
                r, q = i // 4, i % 4
                from_cols = pl.ds(pl.multiple_of(q * part + k * 512, 512), 512)
                chosen += mm(picks[i], tg[r * 128 : (r + 1) * 128, from_cols])
            pa[:, :, cols] = chosen.astype(BF16).reshape(4, 16, 512)
            return 0

        lax.fori_loop(0, part // 512, pick_a, 0)
        state["la"] = swap(net, pa, ma)

    @step("tokx")
    def _():
        loads[5].wait()
        loads[6].wait()
        state["cx"] = net.sibling(cot.at[c])
        state["tx"] = net.sibling(tok.at[c])

    @step("b.s1")
    def _():
        wait_all(*state["lb"])
        landed = mb[...].reshape(64, part_b)
        for q in range(4):
            sb[c, x, y, :, q * part_b : (q + 1) * part_b] = mm(fold(q, (16, 64), 0), landed).astype(BF16)
        gather_b.s1()

    @step("a.s1")
    def _():
        wait_all(*state["la"])
        landed = ma[...].reshape(64, part)
        for q in range(4):
            sa[c, x, y, :, q * part : (q + 1) * part] = mm(fold(q, (16, 64), 0), landed).astype(BF16)
        gather_a.s1()

    pieces = [(0, 0, 4), (1, 0, 4), (2, 0, 4), (3, 0, 2), (3, 2, 2)]
    ring, ring_far, passed, stores = {}, {}, {}, []

    def slab_of(n, dz, cols=ALL):
        k, first, count = pieces[n]
        return w.at[c, k, pl.ds(first, count), rows_of(dz), cols]

    def z_start(n):
        own = slab_of(n, 0)
        ring[n] = net.send(own, own, net.at(dz=1)), net.send(own, own, net.at(dz=-1))
        ring_far[n], passed[n] = net.place(), net.place()
        net.sibling(own, passed[n])

    def z_forward(n):
        side = out_width // 2
        plus, minus = ring[n]
        plus.wait_recv()
        one = slab_of(n, -1, pl.ds(0, side))
        net.send(one, one, net.at(dz=1), ring_far[n])
        minus.wait_recv()
        two = slab_of(n, 1, pl.ds(side, side))
        net.send(two, two, net.at(dz=-1), ring_far[n])
        net.sibling(slab_of(n, -1), passed[n])
        net.sibling(slab_of(n, 1), passed[n])

    def z_end(n):
        last = slab_of(n, 2)
        wait_all(last, ring_far[n])
        net.sibling(last, passed[n])

    def multiply(n, i):
        k, first, count = pieces[n]
        if i == 0:
            wait_all(w.at[1 - c, k, pl.ds(first, count), pl.ds(SHARED, 256 - SHARED)], passed[n])
        count //= 2
        first += i * count

        def block(j, _):
            start = pl.multiple_of((k * RING + j) * 512, 512)
            one, two = w[0, k, j], w[1, k, j]
            cols, lo, hi = pl.ds(start, 512), pl.ds(start, 256), pl.ds(start + 256, 256)
            total[...] += mm(tok[c, :, lo], one) + mm(tok[c, :, hi], two)
            from_a = mm(back[...], sa[:, :, :, :, cols].reshape(512, 512))
            tg[:, lo] = (mm_last(cot[c], one) + from_a[:, :256]).astype(BF16)
            tg[:, hi] = (mm_last(cot[c], two) + from_a[:, 256:]).astype(BF16)
            return 0

        lax.fori_loop(first, first + count, block, 0)
        cols = pl.ds((k * RING + first) * 512, count * 512)
        store = pltpu.make_async_copy(tg.at[:, cols], token_grad.at[:, cols], local_sems.at[7 + len(stores)])
        store.start()
        stores.append(store)

    for n in range(len(pieces)):
        steps["z%d.go" % n] = lambda n=n: z_start(n)
        steps["z%d.fw" % n] = lambda n=n: z_forward(n)
        steps["z%d.en" % n] = lambda n=n: z_end(n)
        for i in range(2):
            steps["m%d.%d" % (n, i)] = lambda n=n, i=i: multiply(n, i)

    stack_b = lambda: sb[...].reshape(512, out_width)

    @step("back")
    def _():
        found = SCALE * mask[...] * mm_last(cot[c], stack_b())
        back[...] = found.astype(BF16)
        back_t[...] = found.T.astype(BF16).reshape(2, 256, rows)
        state["bx"] = net.send(back_t.at[1 - c], back_x, net.at(dc=1))

    def terms_a(i):
        if i == 0:
            state["tx"].wait_recv()
            state["cx"].wait_recv()
            state["bx"].wait_recv()

        def chunk(k, _):
            cols = pl.ds(pl.multiple_of(k * 512, 512), 512)
            found = mm(back_t[c], tok[c, :, cols]) + mm(back_x[...], tok[1 - c, :, cols])
            t_a[:, :, :, cols] = (found * row_scale).astype(BF16).reshape(4, 4, 16, 512)
            return 0

        count = width // 2048
        lax.fori_loop(i * count, (i + 1) * count, chunk, 0)

    for i in range(4):
        steps["T%d" % i] = lambda i=i: terms_a(i)

    def low_sum(i):
        def chunk(k, acc):
            cols = pl.ds(pl.multiple_of(k * 1024, 1024), 1024)
            return acc + mm_last(tok[c, :, cols], sa[:, :, :, :, cols].reshape(512, 1024))

        count = width // 2048
        return lax.fori_loop(i * count, (i + 1) * count, chunk, jnp.zeros((rows, 512), F32))

    @step("low0")
    def _():
        total[:, :512] = low_sum(0)

    @step("low1")
    def _():
        found = mask[...] * (total[:, :512] + low_sum(1))
        low[...] = found.astype(BF16)
        low_t[...] = found.T.astype(BF16).reshape(2, 256, rows)
        state["lx"] = net.send(low_t.at[1 - c], low_x, net.at(dc=1))

    @step("tot")
    def _():
        total[...] = SCALE * mm(low[...], stack_b())

    @step("tb")
    def _():
        state["lx"].wait_recv()
        found = mm(low_t[c], cot[c]) + mm(low_x[...], cot[1 - c])
        t_b[...] = (found * (SCALE * row_scale)).astype(BF16).reshape(4, 4, 16, out_width)

    def unfold(source, target, size):
        found = jnp.zeros((64, size), F32)
        for q in range(4):
            found += mm(fold(q, (64, 16), 1), source[:, q * size : (q + 1) * size])
        target[...] = found.astype(BF16).reshape(4, 16, size)

    @step("unf")
    def _():
        unfold(g_a, na, part)
        unfold(g_b, nb, part_b)

    @step("home")
    def _():
        state["ha"] = swap(net, na, ha)
        state["hb"] = swap(net, nb, hb)

    @step("homw")
    def _():
        wait_all(*state["ha"])
        wait_all(*state["hb"])
        home_a[...] = ha[...].reshape(64, part)
        home_b[...] = hb[...].reshape(64, part_b)

    @step("out")
    def _():
        output[...] = total[...].astype(BF16)

    pl.semaphore_wait(barrier, len(partners))
    for name in ORDER:
        steps[name]()
    for store in stores:
        store.wait()
    for copy in net.started[-SENDS:]:
        copy.wait_send()


def place_kernel(
    slot_table, home_a, home_b, found_output, found_grad, output, token_grad, grad_a, grad_b,
    held, held_grad, held_output, in_sems, out_sems,
):
    rows, owned = token_grad.shape[0], grad_b.shape[0]
    part, part_b = home_a.shape[1], home_b.shape[1]
    z = lax.axis_index("grp")
    count = rows // 8
    bands = [pl.ds(k * count, count) for k in range(8)]
    moves = [(found_grad.at[band], held_grad.at[band], token_grad.at[band]) for band in bands]
    moves.append((found_output, held_output, output))
    loads = [pltpu.make_async_copy(move[0], move[1], in_sems.at[k]) for k, move in enumerate(moves)]
    stores = [pltpu.make_async_copy(move[1], move[2], out_sems.at[k]) for k, move in enumerate(moves)]
    for load in loads:
        load.start()
    row = lax.broadcasted_iota(jnp.int32, (owned, 64), 1)
    adapter = lax.broadcasted_iota(jnp.int32, (owned, 64), 0)
    ids = wanted(slot_table, z, owned, row)
    for i in range(8):
        hits = pick(ids, row, adapter, i)
        cols = pl.ds(i * part, part)
        held[:, cols] = mm(hits, home_a[...]).astype(BF16)
        stores.append(pltpu.make_async_copy(held.at[:, cols], grad_a.at[:, cols], out_sems.at[9 + i]))
        stores[-1].start()
        loads[i].wait()
        stores[i].start()
        grad_b[:, i * part_b : (i + 1) * part_b] = mm(hits, home_b[...]).astype(BF16)
    loads[8].wait()
    stores[8].start()
    for store in stores:
        store.wait()


def local(tokens, tenant, slot_table, weight, adapter_a, adapter_b, cotangent):
    rows, width = tokens.shape
    out_width = weight.shape[1]
    owned = adapter_a.shape[0]
    part, part_b = width // 4, out_width // 4
    vmem, hbm = pl.BlockSpec(memory_space=pltpu.VMEM), pl.BlockSpec(memory_space=pltpu.HBM)
    smem = pl.BlockSpec(memory_space=pltpu.SMEM)
    buffer = lambda *shape, dtype=BF16: pltpu.VMEM(shape, dtype)
    found_output, found_grad, home_a, home_b = pl.pallas_call(
        kernel,
        name="exchange_and_multiply",
        out_shape=(
            jax.ShapeDtypeStruct((rows, out_width), BF16),
            jax.ShapeDtypeStruct((rows, width), BF16),
            jax.ShapeDtypeStruct((64, part), BF16),
            jax.ShapeDtypeStruct((64, part_b), BF16),
        ),
        in_specs=[smem, vmem, hbm, hbm, hbm, hbm, hbm],
        out_specs=(vmem, hbm, vmem, vmem),
        scratch_shapes=[
            buffer(2, 4, 4, 256, out_width),
            buffer(2, 4, 4, 16, width),
            buffer(2, 4, 4, 16, out_width),
            buffer(2, rows, width),
            buffer(2, rows, out_width),
            buffer(rows, width),
            buffer(owned, 2 * out_width),
            buffer(4, 4, 16, width),
            buffer(4, 4, 16, out_width),
            buffer(2, 6, 4, 16, part // 2),
            buffer(2, 6, 16, part // 2),
            buffer(2, 6, 4, 16, part // 2),
            buffer(2, 6, 16, part // 2),
            buffer(2, 6, 4, 16, part_b),
            buffer(2, 6, 16, part_b),
            buffer(16, width),
            buffer(16, out_width),
            buffer(rows, 512, dtype=F32),
            buffer(rows, 512),
            buffer(rows, 512),
            buffer(2, 256, rows),
            buffer(2, 256, rows),
            buffer(256, rows),
            buffer(256, rows),
            buffer(rows, out_width, dtype=F32),
            buffer(4, 16, part),
            buffer(4, 16, part_b),
            buffer(4, 16, part),
            buffer(4, 16, part_b),
            buffer(4, 16, part),
            buffer(4, 16, part_b),
            buffer(4, 16, part),
            buffer(4, 16, part_b),
            pltpu.SemaphoreType.DMA((17,)),
            pltpu.SemaphoreType.DMA((SENDS,)),
            pltpu.SemaphoreType.DMA((RECEIVES,)),
        ],
        compiler_params=pltpu.CompilerParams(
            collective_id=0, has_side_effects=True, vmem_limit_bytes=62 * 1024 * 1024
        ),
    )(slot_table, tenant.reshape(1, rows), tokens, weight, adapter_a, adapter_b, cotangent)

    return pl.pallas_call(
        place_kernel,
        name="place_results",
        out_shape=(
            jax.ShapeDtypeStruct((rows, out_width), BF16),
            jax.ShapeDtypeStruct((rows, width), BF16),
            jax.ShapeDtypeStruct(adapter_a.shape, BF16),
            jax.ShapeDtypeStruct(adapter_b.shape, BF16),
        ),
        in_specs=[smem, vmem, vmem, hbm, hbm],
        out_specs=(hbm, hbm, hbm, vmem),
        scratch_shapes=[
            buffer(owned, 2 * width),
            buffer(rows, width),
            buffer(rows, out_width),
            pltpu.SemaphoreType.DMA((9,)),
            pltpu.SemaphoreType.DMA((17,)),
        ],
        compiler_params=pltpu.CompilerParams(vmem_limit_bytes=62 * 1024 * 1024),
    )(slot_table, home_a, home_b, found_output, found_grad)


def solution(mesh):
    return jax.shard_map(
        local,
        mesh=mesh,
        in_specs=(
            P(("grp", "fsdp"), None),
            P(("grp", "fsdp")),
            P(),
            P("fsdp", None),
            P("grp", "fsdp"),
            P("grp", "fsdp"),
            P(("grp", "fsdp"), None),
        ),
        out_specs=(
            P(("grp", "fsdp"), None),
            P(("grp", "fsdp"), None),
            P("grp", "fsdp"),
            P("grp", "fsdp"),
        ),
        check_vma=False,
    )
```

```python
import math

import jax
import jax.numpy as jnp
from jax import lax
from jax.experimental import pallas as pl
from jax.experimental.pallas import tpu as pltpu
from jax.sharding import PartitionSpec as P

SCALE = 2.0
RING = 4
SENDS = 48
RECEIVES = 128
ORDER = (
    "w.s1", "swapb", "swapa", "d.s1", "tokx", "b.s1", "w.s2", "d.s2", "b.s2", "a.s1", "w.s3", "z0.go",
    "z1.go", "b.s3", "a.s2", "d.s3", "z0.fw", "b.s4", "a.s3", "w.s4", "z2.go", "z3.go", "b.s5", "z1.fw",
    "z4.go", "b.fin", "back", "T0", "z5.go", "z0.en", "d.s4", "T1", "a.s4", "z1.en", "T2", "z2.fw", "r0.s1",
    "a.s5", "z3.fw", "z4.fw", "d.s5", "T3", "z5.fw", "r1.s1", "w.s5", "a.fin", "low0", "z6.go", "z2.en",
    "low1", "d.fin", "r0.s2", "tot", "m2.0", "z3.en", "m0.0", "z7.go", "tb", "q.s1", "r1.s2", "m0.1",
    "m2.1", "m1.0", "z4.en", "m1.1", "z5.en", "m3.0", "q.s2", "m4.0", "z6.fw", "r0.s3", "m4.1", "m5.0",
    "r1.s3", "m5.1", "q.s3", "r0.s4", "z7.fw", "m3.1", "r1.s4", "z6.en", "q.s4", "r0.s5", "hom0", "m6.0",
    "r1.s5", "hom1", "q.s5", "z7.en", "homb", "m6.1", "m7.0", "m7.1", "homw", "out",
)
SHARED = 16
OFFSETS = (0, -1, 1, 2)
MESH = pl.DeviceIdType.MESH
ALL = slice(None)
BF16 = jnp.bfloat16
F32 = jnp.float32


def mod(value):
    return lax.rem(value + RING, RING)


def mm(left, right):
    return jnp.dot(left, right, preferred_element_type=F32)


def mm_last(left, right):
    return lax.dot_general(left, right, (((1,), (1,)), ((), ())), preferred_element_type=F32)


def mm_first(left, right):
    return lax.dot_general(left, right, (((0,), (0,)), ((), ())), preferred_element_type=F32)


class Net:
    def __init__(self, send_sems, recv_sems):
        self.z = lax.axis_index("grp")
        part = lax.axis_index("fsdp")
        self.c = lax.rem(part, 2)
        self.y = lax.rem(part // 2, RING)
        self.x = part // (2 * RING)
        self.send_sems, self.recv_sems, self.started, self.places = send_sems, recv_sems, [], 0

    def at(self, dx=0, dy=0, dz=0, dc=0):
        x, y, z = mod(self.x + dx), mod(self.y + dy), mod(self.z + dz)
        c = lax.rem(self.c + dc, 2)
        return (z, (x * RING + y) * 2 + c)

    def plane(self, axis, step):
        return self.at(dx=step) if axis == 0 else self.at(dy=step)

    def place(self):
        self.places += 1
        return self.recv_sems.at[self.places - 1]

    def send(self, source, target, device, sem=None):
        k = len(self.started)
        if k >= SENDS:
            self.started[k - SENDS].wait_send()
        copy = pltpu.make_async_remote_copy(
            src_ref=source,
            dst_ref=target,
            send_sem=self.send_sems.at[k % SENDS],
            recv_sem=self.place() if sem is None else sem,
            device_id=device,
            device_id_type=MESH,
        )
        copy.start()
        self.started.append(copy)
        return copy

    def sibling(self, ref, sem=None):
        return self.send(ref, ref, self.at(dc=1), sem)


def wait_all(region, sem):
    pltpu.make_async_copy(region, region, sem).wait()


class Gather:
    def __init__(self, net, ref, cut, to_sibling=True):
        self.net, self.buffer, self.cut = net, ref, cut
        self.near, self.line = {}, {}
        self.far = [net.place(), net.place()]
        self.rest = [net.place(), net.place()]
        self.passed = net.place() if to_sibling else None

    def ref(self, half, p, s, part, count):
        x, y = (p, s) if half == 0 else (s, p)
        return self.buffer.at[(self.net.c, x, y) + self.cut(half, part, count)]

    def at(self, half):
        return (self.net.x, self.net.y) if half == 0 else (self.net.y, self.net.x)

    def move(self, ref, axis, step, sem=None):
        return self.net.send(ref, ref, self.net.plane(axis, step), sem)

    def hand(self, ref):
        if self.passed is not None:
            self.net.sibling(ref, self.passed)

    def s1(self):
        for half in (0, 1):
            p, s = self.at(half)
            own = self.ref(half, p, s, 0, 2)
            self.near[half] = self.move(own, half, 1), self.move(own, half, -1)

    def s2(self):
        for half in (0, 1):
            p, s = self.at(half)
            plus, minus = self.near[half]
            plus.wait_recv()
            self.move(self.ref(half, mod(p - 1), s, 0, 1), half, 1, self.far[half])
            minus.wait_recv()
            self.move(self.ref(half, mod(p + 1), s, 1, 1), half, -1, self.far[half])

    def s3(self):
        for half in (0, 1):
            p, s = self.at(half)
            wait_all(self.ref(half, mod(p + 2), s, 0, 2), self.far[half])
            own = self.ref(half, ALL, s, 0, 2)
            self.line[half] = self.move(own, 1 - half, 1), self.move(own, 1 - half, -1)
            self.hand(own)

    def s4(self):
        for half in (0, 1):
            _, s = self.at(half)
            plus, minus = self.line[half]
            plus.wait_recv()
            self.move(self.ref(half, ALL, mod(s - 1), 0, 1), 1 - half, 1, self.rest[half])
            minus.wait_recv()
            self.move(self.ref(half, ALL, mod(s + 1), 1, 1), 1 - half, -1, self.rest[half])
            self.hand(self.ref(half, ALL, mod(s - 1), 0, 2))
            self.hand(self.ref(half, ALL, mod(s + 1), 0, 2))

    def s5(self):
        for half in (0, 1):
            _, s = self.at(half)
            last = self.ref(half, ALL, mod(s + 2), 0, 2)
            wait_all(last, self.rest[half])
            self.hand(last)

    def fin(self):
        wait_all(self.buffer.at[(1 - self.net.c, ALL, ALL) + self.cut(None, 0, 2)], self.passed)


class Scatter:
    def __init__(self, net, terms, line_slots, block_slots, out, cols):
        self.net, self.terms, self.out, self.cols = net, terms, out, cols
        self.line_slots, self.block_slots = line_slots, block_slots
        self.sems = [[[net.place() for _ in range(3)] for _ in range(2)] for _ in range(2)]

    def index(self, half, p, s, part):
        x, y = (p, s) if half == 0 else (s, p)
        return x, y, ALL, self.cols(half, part)

    def at(self, half):
        return (self.net.x, self.net.y) if half == 0 else (self.net.y, self.net.x)

    def first(self, half, slots, axis, block, sems):
        me = self.net.x if axis == 0 else self.net.y
        ahead, behind = self.net.plane(axis, 1), self.net.plane(axis, -1)
        at, slots, net = self.terms.at, slots.at, self.net
        net.send(at[block(mod(me + 2), 0)], slots[half, 0], ahead, sems[0])
        net.send(at[block(mod(me + 2), 1)], slots[half, 1], behind, sems[1])
        net.send(at[block(mod(me + 1), 1)], slots[half, 2], ahead, sems[2])
        net.send(at[block(mod(me - 1), 0)], slots[half, 3], behind, sems[2])

    def add(self, block, slots):
        total = self.terms[block].astype(F32)
        for slot in slots:
            total = total + slot.astype(F32)
        return total

    def s1(self):
        for half in (0, 1):
            self.first(
                half,
                self.line_slots,
                half,
                lambda p, part, h=half: self.index(h, p, ALL, part),
                self.sems[0][half],
            )

    def s2(self):
        for half in (0, 1):
            p, _ = self.at(half)
            sems = self.sems[0][half]
            for k, step in ((0, 1), (1, -1)):
                wait_all(self.line_slots.at[half, k], sems[k])
                target = mod(p + step)

                def line(i, _, half=half, k=k, target=target):
                    block = self.index(half, target, i, k)
                    self.terms[block] = self.add(block, [self.line_slots[half, k, i]]).astype(BF16)
                    return 0

                lax.fori_loop(0, RING, line, 0)
                self.net.send(
                    self.terms.at[self.index(half, target, ALL, k)],
                    self.line_slots.at[half, 4 + k],
                    self.net.plane(half, step),
                    sems[2],
                )

    def s3(self):
        for half in (0, 1):
            p, _ = self.at(half)
            wait_all(self.line_slots.at[half, pl.ds(2, 4)], self.sems[0][half][2])
            for part in (0, 1):

                def line(i, _, half=half, part=part, p=p):
                    block = self.index(half, p, i, part)
                    slots = [self.line_slots[half, 4 + part, i], self.line_slots[half, 3 - part, i]]
                    self.terms[block] = self.add(block, slots).astype(BF16)
                    return 0

                lax.fori_loop(0, RING, line, 0)
            self.first(
                half,
                self.block_slots,
                1 - half,
                lambda s, part, h=half, p=p: self.index(h, p, s, part),
                self.sems[1][half],
            )

    def s4(self):
        for half in (0, 1):
            p, s = self.at(half)
            sems = self.sems[1][half]
            for k, step in ((0, 1), (1, -1)):
                wait_all(self.block_slots.at[half, k], sems[k])
                block = self.index(half, p, mod(s + step), k)
                self.terms[block] = self.add(block, [self.block_slots[half, k]]).astype(BF16)
                self.net.send(
                    self.terms.at[block],
                    self.block_slots.at[half, 4 + k],
                    self.net.plane(1 - half, step),
                    sems[2],
                )

    def s5(self):
        for half in (0, 1):
            p, s = self.at(half)
            wait_all(self.block_slots.at[half, pl.ds(2, 4)], self.sems[1][half][2])
            for part in (0, 1):
                block = self.index(half, p, s, part)
                slots = [self.block_slots[half, 4 + part], self.block_slots[half, 3 - part]]
                self.out[:, self.cols(half, part)] = self.add(block, slots).astype(BF16)


def swap(net, source, landed):
    sem = net.place()
    for step in (1, 3, 2):
        net.send(source.at[mod(net.z + step)], landed.at[net.z], net.at(dz=step), sem)
    landed[net.z] = source[net.z]
    return landed.at[pl.ds(0, 3)], sem


def fold(q, shape, row_dim):
    row = lax.broadcasted_iota(jnp.int32, shape, row_dim)
    col = lax.broadcasted_iota(jnp.int32, shape, 1 - row_dim)
    same = (row // 4 == col // 16) & (row % 4 == col % 4) & ((col // 4) % 4 == q)
    return jnp.where(same, 1.0, 0.0).astype(BF16)


def wanted(slot_table, z, owned, row):
    found = jnp.zeros(row.shape, jnp.int32)
    for g in range(4):
        for j in range(2):
            here = (row // 16 == g) & ((row // 2) % 2 == j)
            found = found + jnp.where(here, slot_table[g, 2 * z + j] - z * owned, 0)
    return found


def pick(ids, row, adapter, i):
    here = (ids == adapter) & ((row % 2) * 4 + (row // 4) % 4 == i)
    return jnp.where(here, 1.0, 0.0).astype(BF16)


def kernel(
    slot_table, tenant, tokens, weight, adapter_a, adapter_b, cotangent,
    output, token_grad, home_a, home_b,
    w, sa, sb, tok, cot, tg, ab, t_a, t_b, lx_0, ly_0, lx_1, ly_1, lx_b, ly_b, g_a, g_b,
    mask, back, low, back_t, low_t, back_x, low_x, total, pa, pb, ma, mb, ha, hb, na, nb,
    local_sems, send_sems, recv_sems,
):
    net = Net(send_sems, recv_sems)
    x, y, z, c = net.x, net.y, net.z, net.c
    width, out_width = tokens.shape[1], weight.shape[1]
    rows = tokens.shape[0]
    owned = adapter_a.shape[0]
    part_a, part_b = width // 4, out_width // 4
    row_scale = 1.0 / math.sqrt(rows * 2 * RING * RING)
    shared, rest, quarter = pl.ds(0, SHARED), pl.ds(SHARED, 128 - SHARED), out_width // 4

    def slab_cols(dz, part=0, count=2):
        start = mod(z + dz) * quarter + part * (quarter // 2)
        return pl.ds(pl.multiple_of(start, quarter // 2), count * (quarter // 2))

    loads = []

    def load(source, target):
        loads.append(pltpu.make_async_copy(source, target, local_sems.at[len(loads)]))
        loads[-1].start()

    for h in (0, 1):
        load(weight.at[pl.ds(h * 128 + SHARED, 128 - SHARED), slab_cols(0)], w.at[c, x, y, h, rest, slab_cols(0)])
    for h in (0, 1):
        load(weight.at[pl.ds(h * 128, SHARED)], w.at[c, x, y, h, shared])
    load(adapter_b, ab)
    for r in (0, 1):
        load(adapter_a.at[:, pl.ds(r * width, width)], tg.at[pl.ds(r * 128, 128)])
    load(cotangent, cot.at[c])
    load(tokens, tok.at[c])

    barrier = pltpu.get_barrier_semaphore()
    partners = [net.at(dx=1), net.at(dx=-1), net.at(dy=1), net.at(dy=-1), net.at(dz=1), net.at(dz=-1)]
    partners += [net.at(dz=2), net.at(dc=1)]
    for device in partners:
        pl.semaphore_signal(barrier, inc=1, device_id=device, device_id_type=MESH)

    steps, state = {}, {}

    def step(name):
        def keep(function):
            steps[name] = function
            return function

        return keep

    def stages(name, collective):
        for stage in ("s1", "s2", "s3", "s4", "s5", "fin"):
            if hasattr(collective, stage):
                steps[name + "." + stage] = getattr(collective, stage)

    def cut_cols(width):
        def cut(half, part, count):
            return ALL, ALL if half is None else pl.ds((half * 2 + part) * (width // 4), count * (width // 4))

        return cut

    def cut_slab(half, part, count):
        return half, rest, slab_cols(0, part, count)

    def cut_shared(half, part, count):
        return ALL if half is None else half, shared, pl.ds(part * (out_width // 2), count * (out_width // 2))

    gather_w = Gather(net, w, cut_slab, to_sibling=False)
    gather_d = Gather(net, w, cut_shared)
    gather_a = Gather(net, sa, cut_cols(width))
    gather_b = Gather(net, sb, cut_cols(out_width))
    stages("w", gather_w)
    stages("d", gather_d)
    stages("a", gather_a)
    stages("b", gather_b)

    def wave(v):
        return lambda half, part: pl.ds((half * 2 + part) * part_a + v * (part_a // 2), part_a // 2)

    stages("r0", Scatter(net, t_a, lx_0, ly_0, g_a, wave(0)))
    stages("r1", Scatter(net, t_a, lx_1, ly_1, g_a, wave(1)))
    stages("q", Scatter(net, t_b, lx_b, ly_b, g_b, lambda half, part: pl.ds((half * 2 + part) * part_b, part_b)))

    row = lax.broadcasted_iota(jnp.int32, (64, owned), 0)
    adapter = lax.broadcasted_iota(jnp.int32, (64, owned), 1)
    ids = wanted(slot_table, z, owned, row)
    picks = [pick(ids, row, adapter, i) for i in range(8)]
    slot = lax.broadcasted_iota(jnp.int32, (16, rows), 0) // 2
    slot_ids = jnp.zeros((16, rows), jnp.int32)
    for s in range(8):
        slot_ids = slot_ids + jnp.where(slot == s, slot_table[z, s], 0)
    hit = jnp.where(slot_ids == tenant[...], 1.0, 0.0)
    mask[...] = jnp.concatenate([hit] * 32, axis=0).T
    for copy in loads[:5]:
        copy.wait()
    chosen = jnp.zeros((64, part_b), F32)
    for i in range(8):
        chosen += mm(picks[i], ab[:, i * part_b : (i + 1) * part_b])
    pb[...] = chosen.astype(BF16).reshape(pb.shape)

    @step("swapb")
    def _():
        state["lb"] = swap(net, pb, mb)

    @step("swapa")
    def _():
        loads[5].wait()
        loads[6].wait()

        def pick_a(k, _):
            cols = pl.ds(pl.multiple_of(k * 512, 512), 512)
            chosen = jnp.zeros((64, 512), F32)
            for i in range(8):
                r, q = i // 4, i % 4
                from_cols = pl.ds(pl.multiple_of(q * part_a + k * 512, 512), 512)
                chosen += mm(picks[i], tg[r * 128 : (r + 1) * 128, from_cols])
            pa[:, :, cols] = chosen.astype(BF16).reshape(4, 16, 512)
            return 0

        lax.fori_loop(0, part_a // 512, pick_a, 0)
        state["la"] = swap(net, pa, ma)

    @step("tokx")
    def _():
        loads[7].wait()
        loads[8].wait()
        state["cx"] = net.sibling(cot.at[c])
        state["tx"] = net.sibling(tok.at[c])

    @step("b.s1")
    def _():
        wait_all(*state["lb"])
        landed = mb[...].reshape(64, part_b)
        for q in range(4):
            sb[c, x, y, :, q * part_b : (q + 1) * part_b] = mm(fold(q, (16, 64), 0), landed).astype(BF16)
        gather_b.s1()

    @step("a.s1")
    def _():
        wait_all(*state["la"])
        landed = ma[...].reshape(64, part_a)
        for q in range(4):
            sa[c, x, y, :, q * part_a : (q + 1) * part_a] = mm(fold(q, (16, 64), 0), landed).astype(BF16)
        gather_a.s1()

    ring, ring_far, passed, stored = {}, {}, {}, {}

    def place_of(n, i):
        offset, h = OFFSETS[n // 2], n % 2
        return (i, mod(y + offset)) if h == 0 else (mod(x + offset), i)

    def slab_of(n, cols):
        return w.at[(c,) + place_of(n, ALL) + (n % 2, rest, cols)]

    def z_start(n):
        own = slab_of(n, slab_cols(0))
        ring[n] = net.send(own, own, net.at(dz=1)), net.send(own, own, net.at(dz=-1))
        ring_far[n], passed[n] = net.place(), net.place()
        net.sibling(own, passed[n])

    def z_forward(n):
        plus, minus = ring[n]
        plus.wait_recv()
        one = slab_of(n, slab_cols(-1, 0, 1))
        net.send(one, one, net.at(dz=1), ring_far[n])
        minus.wait_recv()
        two = slab_of(n, slab_cols(1, 1, 1))
        net.send(two, two, net.at(dz=-1), ring_far[n])
        net.sibling(slab_of(n, slab_cols(-1)), passed[n])
        net.sibling(slab_of(n, slab_cols(1)), passed[n])

    def z_end(n):
        last = slab_of(n, slab_cols(2))
        wait_all(last, ring_far[n])
        net.sibling(last, passed[n])

    def multiply(n, i):
        h = n % 2
        if i == 0:
            wait_all(w.at[(1 - c,) + place_of(n, ALL) + (h, rest)], passed[n])
        places = [place_of(n, 2 * i), place_of(n, 2 * i + 1)]
        cols, blocks = [], []
        for px, py in places:
            for core in (0, 1):
                start = ((px * RING + py) * 2 + core) * 256 + h * 128
                cols.append(pl.ds(pl.multiple_of(start, 128), 128))
                blocks.append(w[core, px, py, h])
        block = jnp.concatenate(blocks, axis=0)
        total[...] += mm(jnp.concatenate([tok[c, :, at] for at in cols], axis=1), block)
        from_a = mm(back[...], jnp.concatenate([sa[:, :, :, :, at].reshape(512, 128) for at in cols], axis=1))
        found = (mm_last(cot[c], block) + from_a).astype(BF16)
        for k, at in enumerate(cols):
            tg[:, at] = found[:, k * 128 : (k + 1) * 128]
            pltpu.make_async_copy(tg.at[:, at], token_grad.at[:, at], local_sems.at[n]).start()

    for n in range(8):
        steps["z%d.go" % n] = lambda n=n: z_start(n)
        steps["z%d.fw" % n] = lambda n=n: z_forward(n)
        steps["z%d.en" % n] = lambda n=n: z_end(n)
        for i in range(2):
            steps["m%d.%d" % (n, i)] = lambda n=n, i=i: multiply(n, i)

    stack_b = lambda: sb[...].reshape(512, out_width)

    @step("back")
    def _():
        found = SCALE * mask[...] * mm_last(cot[c], stack_b())
        back[...] = found.astype(BF16)
        back_t[...] = found.T.astype(BF16).reshape(2, 256, rows)
        state["bx"] = net.send(back_t.at[1 - c], back_x, net.at(dc=1))

    def terms_a(i):
        if i == 0:
            state["tx"].wait_recv()
            state["cx"].wait_recv()
            state["bx"].wait_recv()

        def chunk(k, _):
            start = (k // 2) * part_a + (i // 2) * (part_a // 2) + (k % 2) * 512
            cols = pl.ds(pl.multiple_of(start, 512), 512)
            found = mm(back_t[c], tok[c, :, cols]) + mm(back_x[...], tok[1 - c, :, cols])
            t_a[:, :, :, cols] = (found * row_scale).astype(BF16).reshape(4, 4, 16, 512)
            return 0

        count = width // 2048
        lax.fori_loop(i % 2 * count, (i % 2 + 1) * count, chunk, 0)

    for i in range(4):
        steps["T%d" % i] = lambda i=i: terms_a(i)

    def low_sum(i):
        def chunk(k, acc):
            cols = pl.ds(pl.multiple_of(k * 1024, 1024), 1024)
            return acc + mm_last(tok[c, :, cols], sa[:, :, :, :, cols].reshape(512, 1024))

        count = width // 2048
        return lax.fori_loop(i * count, (i + 1) * count, chunk, jnp.zeros((rows, 512), F32))

    @step("low0")
    def _():
        total[:, :512] = low_sum(0)

    @step("low1")
    def _():
        found = mask[...] * (total[:, :512] + low_sum(1))
        low[...] = found.astype(BF16)
        low_t[...] = found.T.astype(BF16).reshape(2, 256, rows)
        state["lx"] = net.send(low_t.at[1 - c], low_x, net.at(dc=1))

    @step("tot")
    def _():
        total[...] = SCALE * mm(low[...], stack_b())

    @step("tb")
    def _():
        state["lx"].wait_recv()
        found = mm(low_t[c], cot[c]) + mm(low_x[...], cot[1 - c])
        t_b[...] = (found * (SCALE * row_scale)).astype(BF16).reshape(4, 4, 16, out_width)

    def unfold(source, size, start, count):
        found = jnp.zeros((64, count), F32)
        for q in range(4):
            found += mm(fold(q, (64, 16), 1), source[:, q * size + start : q * size + start + count])
        return found.astype(BF16).reshape(4, 16, count)

    def go_home(v):
        cols = pl.ds(v * (part_a // 2), part_a // 2)
        na[:, :, cols] = unfold(g_a, part_a, v * (part_a // 2), part_a // 2)
        state["ha%d" % v] = swap(net, na.at[:, :, cols], ha.at[:, :, cols])

    steps["hom0"] = lambda: go_home(0)
    steps["hom1"] = lambda: go_home(1)

    @step("homb")
    def _():
        nb[...] = unfold(g_b, part_b, 0, part_b)
        state["hb"] = swap(net, nb, hb)

    @step("homw")
    def _():
        wait_all(*state["ha0"])
        wait_all(*state["ha1"])
        wait_all(*state["hb"])
        home_a[...] = ha[...].reshape(64, part_a)
        home_b[...] = hb[...].reshape(64, part_b)

    @step("out")
    def _():
        output[...] = total[...].astype(BF16)

    pl.semaphore_wait(barrier, len(partners))
    for name in ORDER:
        steps[name]()
    for n in range(8):
        wait_all(tg.at[:, pl.ds(0, 1024)], local_sems.at[n])
    for copy in net.started[-SENDS:]:
        copy.wait_send()


def place_kernel(
    slot_table, home_a, home_b, found_output, found_grad, output, token_grad, grad_a, grad_b,
    ha, hb, held, held_b, held_grad, held_output, in_sems, out_sems,
):
    rows, owned = token_grad.shape[0], grad_b.shape[0]
    part = home_a.shape[1]
    z = lax.axis_index("grp")
    count = rows // 4
    bands = [pl.ds(k * count, count) for k in range(4)]
    moves = [(home_a, ha, None), (home_b, hb, None)]
    moves += [(found_grad.at[band], held_grad.at[band], token_grad.at[band]) for band in bands]
    moves.append((found_output, held_output, output))
    loads = [pltpu.make_async_copy(move[0], move[1], in_sems.at[k]) for k, move in enumerate(moves)]
    for load in loads:
        load.start()
    stores = []

    def store(source, target):
        stores.append(pltpu.make_async_copy(source, target, out_sems.at[len(stores)]))
        stores[-1].start()

    row = lax.broadcasted_iota(jnp.int32, (owned, 64), 1)
    adapter = lax.broadcasted_iota(jnp.int32, (owned, 64), 0)
    ids = wanted(slot_table, z, owned, row)
    loads[0].wait()
    for i in range(8):
        cols = pl.ds(i * part, part)
        held[:, cols] = mm(pick(ids, row, adapter, i), ha[...]).astype(BF16)
        store(held.at[:, cols], grad_a.at[:, cols])
        if i == 1:
            for load, (_, source, target) in zip(loads[2:], moves[2:]):
                load.wait()
                store(source, target)
    loads[1].wait()
    line = lax.broadcasted_iota(jnp.int32, hb.shape, 0)
    piece = (line % 2) * 4 + (line // 4) % 4
    spread = jnp.concatenate([jnp.where(piece == i, hb[...], 0.0) for i in range(8)], axis=1)
    hits = jnp.where(ids == adapter, 1.0, 0.0).astype(BF16)
    held_b[...] = mm(hits, spread.astype(BF16)).astype(BF16)
    store(held_b, grad_b)
    for copy in stores:
        copy.wait()


def local(tokens, tenant, slot_table, weight, adapter_a, adapter_b, cotangent):
    rows, width = tokens.shape
    out_width = weight.shape[1]
    owned = adapter_a.shape[0]
    part, part_b = width // 4, out_width // 4
    vmem, hbm = pl.BlockSpec(memory_space=pltpu.VMEM), pl.BlockSpec(memory_space=pltpu.HBM)
    smem = pl.BlockSpec(memory_space=pltpu.SMEM)
    buffer = lambda *shape, dtype=BF16: pltpu.VMEM(shape, dtype)
    found_output, found_grad, home_a, home_b = pl.pallas_call(
        kernel,
        name="exchange_and_multiply",
        out_shape=(
            jax.ShapeDtypeStruct((rows, out_width), BF16),
            jax.ShapeDtypeStruct((rows, width), BF16),
            jax.ShapeDtypeStruct((64, part), BF16),
            jax.ShapeDtypeStruct((64, part_b), BF16),
        ),
        in_specs=[smem, vmem, hbm, hbm, hbm, hbm, hbm],
        out_specs=(vmem, hbm, vmem, vmem),
        scratch_shapes=[
            buffer(2, 4, 4, 2, 128, out_width),
            buffer(2, 4, 4, 16, width),
            buffer(2, 4, 4, 16, out_width),
            buffer(2, rows, width),
            buffer(2, rows, out_width),
            buffer(rows, width),
            buffer(owned, 2 * out_width),
            buffer(4, 4, 16, width),
            buffer(4, 4, 16, out_width),
            buffer(2, 6, 4, 16, part // 2),
            buffer(2, 6, 16, part // 2),
            buffer(2, 6, 4, 16, part // 2),
            buffer(2, 6, 16, part // 2),
            buffer(2, 6, 4, 16, part_b),
            buffer(2, 6, 16, part_b),
            buffer(16, width),
            buffer(16, out_width),
            buffer(rows, 512, dtype=F32),
            buffer(rows, 512),
            buffer(rows, 512),
            buffer(2, 256, rows),
            buffer(2, 256, rows),
            buffer(256, rows),
            buffer(256, rows),
            buffer(rows, out_width, dtype=F32),
            buffer(4, 16, part),
            buffer(4, 16, part_b),
            buffer(4, 16, part),
            buffer(4, 16, part_b),
            buffer(4, 16, part),
            buffer(4, 16, part_b),
            buffer(4, 16, part),
            buffer(4, 16, part_b),
            pltpu.SemaphoreType.DMA((9,)),
            pltpu.SemaphoreType.DMA((SENDS,)),
            pltpu.SemaphoreType.DMA((RECEIVES,)),
        ],
        compiler_params=pltpu.CompilerParams(
            collective_id=0, has_side_effects=True, vmem_limit_bytes=62 * 1024 * 1024
        ),
    )(slot_table, tenant.reshape(1, rows), tokens, weight, adapter_a, adapter_b, cotangent)

    return pl.pallas_call(
        place_kernel,
        name="place_results",
        out_shape=(
            jax.ShapeDtypeStruct((rows, out_width), BF16),
            jax.ShapeDtypeStruct((rows, width), BF16),
            jax.ShapeDtypeStruct(adapter_a.shape, BF16),
            jax.ShapeDtypeStruct(adapter_b.shape, BF16),
        ),
        in_specs=[smem, hbm, hbm, hbm, hbm],
        out_specs=(hbm, hbm, hbm, hbm),
        scratch_shapes=[
            buffer(64, part),
            buffer(64, part_b),
            buffer(owned, 2 * width),
            buffer(owned, 2 * out_width),
            buffer(rows, width),
            buffer(rows, out_width),
            pltpu.SemaphoreType.DMA((7,)),
            pltpu.SemaphoreType.DMA((14,)),
        ],
        compiler_params=pltpu.CompilerParams(vmem_limit_bytes=62 * 1024 * 1024),
    )(slot_table, home_a, home_b, found_output, found_grad)


def solution(mesh):
    return jax.shard_map(
        local,
        mesh=mesh,
        in_specs=(
            P(("grp", "fsdp"), None),
            P(("grp", "fsdp")),
            P(),
            P("fsdp", None),
            P("grp", "fsdp"),
            P("grp", "fsdp"),
            P(("grp", "fsdp"), None),
        ),
        out_specs=(
            P(("grp", "fsdp"), None),
            P(("grp", "fsdp"), None),
            P("grp", "fsdp"),
            P("grp", "fsdp"),
        ),
        check_vma=False,
    )
```

```python
import math

import jax
import jax.numpy as jnp
from jax import lax
from jax.experimental import pallas as pl
from jax.experimental.pallas import tpu as pltpu
from jax.sharding import PartitionSpec as P

SCALE = 2.0
RING = 4
SENDS = 40
RECEIVES = 92
ORDER = (
    "w.s1", "swapb", "swapa", "d.s1", "b.s1", "tokx", "mask", "w.s2", "d.s2", "a.s1", "b.s2", "w.s3", "z0.go",
    "z1.go", "b.s3", "a.s2", "d.s3", "z0.fw", "b.s4", "a.s3", "w.s4", "z2.go", "z0.en", "b.s5", "z3.go",
    "d.s4", "z1.fw", "z2.fw", "z4.go", "b.fin", "back", "T0", "a.s4", "T1", "T2", "d.s5", "z5.go", "T3",
    "z1.en", "r1.s1", "r0.s1", "w.s5", "d.fin", "z2.en", "o1.0", "o2.0", "z3.fw", "o0.0", "o1.1", "z4.fw",
    "a.s5", "o0.1", "a.fin", "z6.go", "low0", "low1", "r1.s2", "z3.en", "x0.0", "x1.0", "z4.en", "z5.fw",
    "tb", "q.s1", "x2.0", "o4.0", "o3.0", "z7.go", "r0.s2", "x3.0", "x0.1", "x4.0", "x3.1", "q.s2", "r1.s3",
    "z5.en", "o2.1", "o3.1", "x1.1", "z6.fw", "x2.1", "r0.s3", "o5.0", "q.s3", "x4.1", "r1.s4", "tot",
    "z7.fw", "x5.0", "r0.s4", "x5.1", "z6.en", "q.s4", "o4.1", "o5.1", "r1.s5", "hom1", "o6.0", "x6.0",
    "r0.s5", "hom0", "z7.en", "q.s5", "o6.1", "homb", "x6.1", "o7.0", "x7.0", "o7.1", "x7.1", "homw", "out",
)
SHARED = 16
OFFSETS = (0, -1, 1, 2)
MESH = pl.DeviceIdType.MESH
ALL = slice(None)
BF16 = jnp.bfloat16
F32 = jnp.float32


def mod(value):
    return lax.rem(value + RING, RING)


def mm(left, right):
    return jnp.dot(left, right, preferred_element_type=F32)


def mm_last(left, right):
    return lax.dot_general(left, right, (((1,), (1,)), ((), ())), preferred_element_type=F32)


def mm_first(left, right):
    return lax.dot_general(left, right, (((0,), (0,)), ((), ())), preferred_element_type=F32)


class Net:
    def __init__(self, send_sems, recv_sems):
        self.z = lax.axis_index("grp")
        part = lax.axis_index("fsdp")
        self.c = lax.rem(part, 2)
        self.y = lax.rem(part // 2, RING)
        self.x = part // (2 * RING)
        self.send_sems, self.recv_sems, self.started, self.places = send_sems, recv_sems, [], 0

    def at(self, dx=0, dy=0, dz=0, dc=0):
        x, y, z = mod(self.x + dx), mod(self.y + dy), mod(self.z + dz)
        c = lax.rem(self.c + dc, 2)
        return (z, (x * RING + y) * 2 + c)

    def plane(self, axis, step):
        return self.at(dx=step) if axis == 0 else self.at(dy=step)

    def place(self):
        self.places += 1
        return self.recv_sems.at[self.places - 1]

    def send(self, source, target, device, sem=None):
        k = len(self.started)
        if k >= SENDS:
            self.started[k - SENDS].wait_send()
        copy = pltpu.make_async_remote_copy(
            src_ref=source,
            dst_ref=target,
            send_sem=self.send_sems.at[k % SENDS],
            recv_sem=self.place() if sem is None else sem,
            device_id=device,
            device_id_type=MESH,
        )
        copy.start()
        self.started.append(copy)
        return copy

    def sibling(self, ref, sem=None):
        return self.send(ref, ref, self.at(dc=1), sem)


def wait_all(region, sem):
    pltpu.make_async_copy(region, region, sem).wait()


class Gather:
    def __init__(self, net, ref, cut, to_sibling=True):
        self.net, self.buffer, self.cut = net, ref, cut
        self.near, self.far, self.line, self.rest = [[net.place(), net.place()] for _ in range(4)]
        self.passed = net.place() if to_sibling else None

    def ref(self, half, p, s, part, count):
        x, y = (p, s) if half == 0 else (s, p)
        return self.buffer.at[(self.net.c, x, y) + self.cut(half, part, count)]

    def at(self, half):
        return (self.net.x, self.net.y) if half == 0 else (self.net.y, self.net.x)

    def move(self, ref, axis, step, sem=None):
        return self.net.send(ref, ref, self.net.plane(axis, step), sem)

    def hand(self, ref):
        if self.passed is not None:
            self.net.sibling(ref, self.passed)

    def s1(self):
        for half in (0, 1):
            p, s = self.at(half)
            own = self.ref(half, p, s, 0, 2)
            self.move(own, half, 1, self.near[half])
            self.move(own, half, -1, self.near[half])

    def s2(self):
        for half in (0, 1):
            p, s = self.at(half)
            wait_all(self.ref(half, pl.ds(0, 2), s, 0, 2), self.near[half])
            self.move(self.ref(half, mod(p - 1), s, 0, 1), half, 1, self.far[half])
            self.move(self.ref(half, mod(p + 1), s, 1, 1), half, -1, self.far[half])

    def s3(self):
        for half in (0, 1):
            p, s = self.at(half)
            wait_all(self.ref(half, mod(p + 2), s, 0, 2), self.far[half])
            own = self.ref(half, ALL, s, 0, 2)
            self.move(own, 1 - half, 1, self.line[half])
            self.move(own, 1 - half, -1, self.line[half])
            self.hand(own)

    def s4(self):
        for half in (0, 1):
            _, s = self.at(half)
            wait_all(self.ref(half, ALL, pl.ds(0, 2), 0, 2), self.line[half])
            self.move(self.ref(half, ALL, mod(s - 1), 0, 1), 1 - half, 1, self.rest[half])
            self.move(self.ref(half, ALL, mod(s + 1), 1, 1), 1 - half, -1, self.rest[half])
            self.hand(self.ref(half, ALL, mod(s - 1), 0, 2))
            self.hand(self.ref(half, ALL, mod(s + 1), 0, 2))

    def s5(self):
        for half in (0, 1):
            _, s = self.at(half)
            last = self.ref(half, ALL, mod(s + 2), 0, 2)
            wait_all(last, self.rest[half])
            self.hand(last)

    def fin(self):
        wait_all(self.buffer.at[(1 - self.net.c, ALL, ALL) + self.cut(None, 0, 2)], self.passed)


class Scatter:
    def __init__(self, net, terms, line_slots, block_slots, out, cols):
        self.net, self.terms, self.out, self.cols = net, terms, out, cols
        self.line_slots, self.block_slots = line_slots, block_slots
        self.sems = [[[net.place(), net.place()] for _ in range(2)] for _ in range(2)]

    def index(self, half, p, s, part):
        x, y = (p, s) if half == 0 else (s, p)
        return x, y, ALL, self.cols(half, part)

    def at(self, half):
        return (self.net.x, self.net.y) if half == 0 else (self.net.y, self.net.x)

    def first(self, half, slots, axis, block, sems):
        me = self.net.x if axis == 0 else self.net.y
        ahead, behind = self.net.plane(axis, 1), self.net.plane(axis, -1)
        at, slots, net = self.terms.at, slots.at, self.net
        net.send(at[block(mod(me + 2), 0)], slots[half, 0], ahead, sems[0])
        net.send(at[block(mod(me + 2), 1)], slots[half, 1], behind, sems[0])
        net.send(at[block(mod(me + 1), 1)], slots[half, 2], ahead, sems[1])
        net.send(at[block(mod(me - 1), 0)], slots[half, 3], behind, sems[1])

    def add(self, block, slots):
        total = self.terms[block].astype(F32)
        for slot in slots:
            total = total + slot.astype(F32)
        return total

    def s1(self):
        for half in (0, 1):
            self.first(
                half,
                self.line_slots,
                half,
                lambda p, part, h=half: self.index(h, p, ALL, part),
                self.sems[0][half],
            )

    def s2(self):
        for half in (0, 1):
            p, _ = self.at(half)
            sems = self.sems[0][half]
            wait_all(self.line_slots.at[half, pl.ds(0, 2)], sems[0])
            for k, step in ((0, 1), (1, -1)):
                target = mod(p + step)

                def line(i, _, half=half, k=k, target=target):
                    block = self.index(half, target, i, k)
                    self.terms[block] = self.add(block, [self.line_slots[half, k, i]]).astype(BF16)
                    return 0

                lax.fori_loop(0, RING, line, 0)
                self.net.send(
                    self.terms.at[self.index(half, target, ALL, k)],
                    self.line_slots.at[half, 4 + k],
                    self.net.plane(half, step),
                    sems[1],
                )

    def s3(self):
        for half in (0, 1):
            p, _ = self.at(half)
            wait_all(self.line_slots.at[half, pl.ds(2, 4)], self.sems[0][half][1])
            for part in (0, 1):

                def line(i, _, half=half, part=part, p=p):
                    block = self.index(half, p, i, part)
                    slots = [self.line_slots[half, 4 + part, i], self.line_slots[half, 3 - part, i]]
                    self.terms[block] = self.add(block, slots).astype(BF16)
                    return 0

                lax.fori_loop(0, RING, line, 0)
            self.first(
                half,
                self.block_slots,
                1 - half,
                lambda s, part, h=half, p=p: self.index(h, p, s, part),
                self.sems[1][half],
            )

    def s4(self):
        for half in (0, 1):
            p, s = self.at(half)
            sems = self.sems[1][half]
            wait_all(self.block_slots.at[half, pl.ds(0, 2)], sems[0])
            for k, step in ((0, 1), (1, -1)):
                block = self.index(half, p, mod(s + step), k)
                self.terms[block] = self.add(block, [self.block_slots[half, k]]).astype(BF16)
                self.net.send(
                    self.terms.at[block],
                    self.block_slots.at[half, 4 + k],
                    self.net.plane(1 - half, step),
                    sems[1],
                )

    def s5(self):
        for half in (0, 1):
            p, s = self.at(half)
            wait_all(self.block_slots.at[half, pl.ds(2, 4)], self.sems[1][half][1])
            for part in (0, 1):
                block = self.index(half, p, s, part)
                slots = [self.block_slots[half, 4 + part], self.block_slots[half, 3 - part]]
                self.out[:, self.cols(half, part)] = self.add(block, slots).astype(BF16)


def swap(net, source, landed):
    sem = net.place()
    for step in (1, 3, 2):
        net.send(source.at[mod(net.z + step)], landed.at[net.z], net.at(dz=step), sem)
    landed[net.z] = source[net.z]
    return landed.at[pl.ds(0, 3)], sem


def fold(q, shape, row_dim):
    row = lax.broadcasted_iota(jnp.int32, shape, row_dim)
    col = lax.broadcasted_iota(jnp.int32, shape, 1 - row_dim)
    same = (row // 4 == col // 16) & (row % 4 == col % 4) & ((col // 4) % 4 == q)
    return jnp.where(same, 1.0, 0.0).astype(BF16)


def wanted(slot_table, z, owned, row):
    found = jnp.zeros(row.shape, jnp.int32)
    for g in range(4):
        for j in range(2):
            here = (row // 16 == g) & ((row // 2) % 2 == j)
            found = found + jnp.where(here, slot_table[g, 2 * z + j] - z * owned, 0)
    return found


def pick(ids, row, adapter, i):
    here = (ids == adapter) & ((row % 2) * 4 + (row // 4) % 4 == i)
    return jnp.where(here, 1.0, 0.0).astype(BF16)


def kernel(
    slot_table, tenant, tokens, weight, adapter_a, adapter_b, cotangent,
    output, token_grad, home_a, home_b,
    w, sa, sb, tok, cot, tg, ab, t_a, t_b, lx_0, ly_0, lx_1, ly_1, lx_b, ly_b, g_a, g_b,
    mask, partial, back, low, back_t, low_t, back_x, low_x, total, held, pa, pb, ma, mb, ha, hb, na, nb,
    local_sems, send_sems, recv_sems,
):
    net = Net(send_sems, recv_sems)
    x, y, z, c = net.x, net.y, net.z, net.c
    width, out_width = tokens.shape[1], weight.shape[1]
    rows = tokens.shape[0]
    owned = adapter_a.shape[0]
    part_a, part_b = width // 4, out_width // 4
    row_scale = 1.0 / math.sqrt(rows * 2 * RING * RING)
    shared, rest, quarter = pl.ds(0, SHARED), pl.ds(SHARED, 128 - SHARED), out_width // 4

    def slab_cols(dz, part=0, count=2):
        start = mod(z + dz) * quarter + part * (quarter // 2)
        return pl.ds(pl.multiple_of(start, quarter // 2), count * (quarter // 2))

    loads = []

    def load(source, target):
        loads.append(pltpu.make_async_copy(source, target, local_sems.at[len(loads)]))
        loads[-1].start()

    for h in (0, 1):
        load(weight.at[pl.ds(h * 128 + SHARED, 128 - SHARED), slab_cols(0)], w.at[c, x, y, h, rest, slab_cols(0)])
    for h in (0, 1):
        load(weight.at[pl.ds(h * 128, SHARED)], w.at[c, x, y, h, shared])
    load(adapter_b, ab)
    for r in (0, 1):
        load(adapter_a.at[:, pl.ds(r * width, width)], tg.at[pl.ds(r * 128, 128)])
    load(cotangent, cot.at[c])
    load(tokens, tok.at[c])

    barrier = pltpu.get_barrier_semaphore()
    partners = [net.at(dx=1), net.at(dx=-1), net.at(dy=1), net.at(dy=-1), net.at(dz=1), net.at(dz=-1)]
    partners += [net.at(dz=2), net.at(dc=1)]
    for device in partners:
        pl.semaphore_signal(barrier, inc=1, device_id=device, device_id_type=MESH)

    steps, state = {}, {}

    def step(name):
        def keep(function):
            steps[name] = function
            return function

        return keep

    def stages(name, collective):
        for stage in ("s1", "s2", "s3", "s4", "s5", "fin"):
            if hasattr(collective, stage):
                steps[name + "." + stage] = getattr(collective, stage)

    def cut_cols(width):
        def cut(half, part, count):
            return ALL, ALL if half is None else pl.ds((half * 2 + part) * (width // 4), count * (width // 4))

        return cut

    def cut_slab(half, part, count):
        return half, rest, slab_cols(0, part, count)

    def cut_shared(half, part, count):
        return ALL if half is None else half, shared, pl.ds(part * (out_width // 2), count * (out_width // 2))

    gather_w = Gather(net, w, cut_slab, to_sibling=False)
    gather_d = Gather(net, w, cut_shared)
    gather_a = Gather(net, sa, cut_cols(width))
    gather_b = Gather(net, sb, cut_cols(out_width))
    stages("w", gather_w)
    stages("d", gather_d)
    stages("a", gather_a)
    stages("b", gather_b)

    def wave(v):
        return lambda half, part: pl.ds((half * 2 + part) * part_a + v * (part_a // 2), part_a // 2)

    stages("r0", Scatter(net, t_a, lx_0, ly_0, g_a, wave(0)))
    stages("r1", Scatter(net, t_a, lx_1, ly_1, g_a, wave(1)))
    stages("q", Scatter(net, t_b, lx_b, ly_b, g_b, lambda half, part: pl.ds((half * 2 + part) * part_b, part_b)))

    @step("w.s1")
    def _():
        loads[0].wait()
        loads[1].wait()
        gather_w.s1()

    @step("d.s1")
    def _():
        loads[2].wait()
        loads[3].wait()
        gather_d.s1()

    def all_picks():
        row = lax.broadcasted_iota(jnp.int32, (64, owned), 0)
        adapter = lax.broadcasted_iota(jnp.int32, (64, owned), 1)
        ids = wanted(slot_table, z, owned, row)
        return [pick(ids, row, adapter, i) for i in range(8)]

    @step("mask")
    def _():
        slot = lax.broadcasted_iota(jnp.int32, (16, rows), 0) // 2
        slot_ids = jnp.zeros((16, rows), jnp.int32)
        for s in range(8):
            slot_ids = slot_ids + jnp.where(slot == s, slot_table[z, s], 0)
        hit = jnp.where(slot_ids == tenant[...], 1.0, 0.0)
        mask[...] = jnp.concatenate([hit] * 32, axis=0).T
        total[...] = jnp.zeros_like(total)

    @step("swapb")
    def _():
        loads[4].wait()
        picks = state["picks"] = all_picks()
        chosen = jnp.zeros((64, part_b), F32)
        for i in range(8):
            chosen += mm(picks[i], ab[:, i * part_b : (i + 1) * part_b])
        pb[...] = chosen.astype(BF16).reshape(pb.shape)
        state["lb"] = swap(net, pb, mb)

    @step("swapa")
    def _():
        loads[5].wait()
        loads[6].wait()
        picks = state["picks"]

        def pick_a(k, _):
            cols = pl.ds(pl.multiple_of(k * 512, 512), 512)
            chosen = jnp.zeros((64, 512), F32)
            for i in range(8):
                r, q = i // 4, i % 4
                from_cols = pl.ds(pl.multiple_of(q * part_a + k * 512, 512), 512)
                chosen += mm(picks[i], tg[r * 128 : (r + 1) * 128, from_cols])
            pa[:, :, cols] = chosen.astype(BF16).reshape(4, 16, 512)
            return 0

        lax.fori_loop(0, part_a // 512, pick_a, 0)
        state["la"] = swap(net, pa, ma)

    @step("tokx")
    def _():
        loads[7].wait()
        loads[8].wait()
        state["cx"] = net.sibling(cot.at[c])
        state["tx"] = net.sibling(tok.at[c])

    @step("b.s1")
    def _():
        wait_all(*state["lb"])
        landed = mb[...].reshape(64, part_b)
        for q in range(4):
            sb[c, x, y, :, q * part_b : (q + 1) * part_b] = mm(fold(q, (16, 64), 0), landed).astype(BF16)
        gather_b.s1()

    @step("a.s1")
    def _():
        wait_all(*state["la"])
        landed = ma[...].reshape(64, part_a)
        for q in range(4):
            sa[c, x, y, :, q * part_a : (q + 1) * part_a] = mm(fold(q, (16, 64), 0), landed).astype(BF16)
        gather_a.s1()

    ring, ring_far, passed, stored = {}, {}, {}, []

    def place_of(n, i):
        offset, h = OFFSETS[n // 2], n % 2
        return (i, mod(y + offset)) if h == 0 else (mod(x + offset), i)

    def slab_of(n, cols):
        return w.at[(c,) + place_of(n, ALL) + (n % 2, rest, cols)]

    def z_start(n):
        own = slab_of(n, slab_cols(0))
        ring[n], ring_far[n], passed[n] = net.place(), net.place(), net.place()
        net.send(own, own, net.at(dz=1), ring[n])
        net.send(own, own, net.at(dz=-1), ring[n])
        net.sibling(own, passed[n])

    def z_forward(n):
        wait_all(w.at[(c,) + place_of(n, ALL) + (n % 2, rest, pl.ds(0, 2 * quarter))], ring[n])
        one = slab_of(n, slab_cols(-1, 0, 1))
        net.send(one, one, net.at(dz=1), ring_far[n])
        two = slab_of(n, slab_cols(1, 1, 1))
        net.send(two, two, net.at(dz=-1), ring_far[n])
        net.sibling(slab_of(n, slab_cols(-1)), passed[n])
        net.sibling(slab_of(n, slab_cols(1)), passed[n])

    def z_end(n):
        last = slab_of(n, slab_cols(2))
        wait_all(last, ring_far[n])
        net.sibling(last, passed[n])

    def blocks_of(n, i):
        h, cols, blocks = n % 2, [], []
        for px, py in (place_of(n, 2 * i), place_of(n, 2 * i + 1)):
            for core in (0, 1):
                start = ((px * RING + py) * 2 + core) * 256 + h * 128
                cols.append(pl.ds(pl.multiple_of(start, 128), 128))
                blocks.append(w[core, px, py, h])
        return cols, jnp.concatenate(blocks, axis=0)

    def multiply_out(n, i):
        if i == 0:
            wait_all(w.at[(1 - c,) + place_of(n, ALL) + (n % 2, rest)], passed[n])
        cols, block = blocks_of(n, i)
        total[...] += mm(jnp.concatenate([tok[c, :, at] for at in cols], axis=1), block)

    def multiply_back(n, i):
        cols, block = blocks_of(n, i)
        from_a = mm(back[...], jnp.concatenate([sa[:, :, :, :, at].reshape(512, 128) for at in cols], axis=1))
        found = (mm_last(cot[c], block) + from_a).astype(BF16)
        for k, at in enumerate(cols):
            tg[:, at] = found[:, k * 128 : (k + 1) * 128]
            pltpu.make_async_copy(tg.at[:, at], token_grad.at[:, at], local_sems.at[n]).start()

    for n in range(8):
        steps["z%d.go" % n] = lambda n=n: z_start(n)
        steps["z%d.fw" % n] = lambda n=n: z_forward(n)
        steps["z%d.en" % n] = lambda n=n: z_end(n)
        for i in range(2):
            steps["o%d.%d" % (n, i)] = lambda n=n, i=i: multiply_out(n, i)
            steps["x%d.%d" % (n, i)] = lambda n=n, i=i: multiply_back(n, i)

    stack_b = lambda: sb[...].reshape(512, out_width)

    @step("back")
    def _():
        found = SCALE * mask[...] * mm_last(cot[c], stack_b())
        back[...] = found.astype(BF16)
        back_t[...] = found.T.astype(BF16).reshape(2, 256, rows)
        state["bx"] = net.send(back_t.at[1 - c], back_x, net.at(dc=1))

    def terms_a(i):
        if i == 0:
            state["tx"].wait_recv()
            state["cx"].wait_recv()
            state["bx"].wait_recv()

        def chunk(k, _):
            start = (k // 2) * part_a + (i // 2) * (part_a // 2) + (k % 2) * 512
            cols = pl.ds(pl.multiple_of(start, 512), 512)
            found = mm(back_t[c], tok[c, :, cols]) + mm(back_x[...], tok[1 - c, :, cols])
            t_a[:, :, :, cols] = (found * row_scale).astype(BF16).reshape(4, 4, 16, 512)
            return 0

        count = width // 2048
        lax.fori_loop(i % 2 * count, (i % 2 + 1) * count, chunk, 0)

    for i in range(4):
        steps["T%d" % i] = lambda i=i: terms_a(i)

    def low_sum(i):
        cols = pl.ds(i * (width // 2), width // 2)
        return mm_last(tok[c, :, cols], sa[:, :, :, :, cols].reshape(512, width // 2))

    @step("low0")
    def _():
        partial[...] = low_sum(0)

    @step("low1")
    def _():
        found = mask[...] * (partial[...] + low_sum(1))
        low[...] = found.astype(BF16)
        low_t[...] = found.T.astype(BF16).reshape(2, 256, rows)
        state["lx"] = net.send(low_t.at[1 - c], low_x, net.at(dc=1))

    @step("tot")
    def _():
        total[...] += SCALE * mm(low[...], stack_b())

    @step("tb")
    def _():
        state["lx"].wait_recv()
        found = mm(low_t[c], cot[c]) + mm(low_x[...], cot[1 - c])
        t_b[...] = (found * (SCALE * row_scale)).astype(BF16).reshape(4, 4, 16, out_width)

    def unfold(source, size, start, count):
        found = jnp.zeros((64, count), F32)
        for q in range(4):
            found += mm(fold(q, (64, 16), 1), source[:, q * size + start : q * size + start + count])
        return found.astype(BF16).reshape(4, 16, count)

    def go_home(v):
        cols = pl.ds(v * (part_a // 2), part_a // 2)
        na[:, :, cols] = unfold(g_a, part_a, v * (part_a // 2), part_a // 2)
        state["ha%d" % v] = swap(net, na.at[:, :, cols], ha.at[:, :, cols])

    steps["hom0"] = lambda: go_home(0)
    steps["hom1"] = lambda: go_home(1)

    def store(source, target, k):
        stored.append(pltpu.make_async_copy(source, target, local_sems.at[k]))
        stored[-1].start()

    @step("homb")
    def _():
        nb[...] = unfold(g_b, part_b, 0, part_b)
        state["hb"] = swap(net, nb, hb)

    @step("homw")
    def _():
        wait_all(*state["ha0"])
        wait_all(*state["ha1"])
        wait_all(*state["hb"])
        store(ha, home_a, 8)
        store(hb, home_b, 9)

    @step("out")
    def _():
        held[...] = total[...].astype(BF16)
        store(held, output, 10)

    pl.semaphore_wait(barrier, len(partners))
    for name in ORDER:
        steps[name]()
    for copy in stored:
        copy.wait()
    for n in range(8):
        wait_all(tg.at[:, pl.ds(0, 1024)], local_sems.at[n])
    for copy in net.started[-SENDS:]:
        copy.wait_send()


def place_kernel(
    slot_table, home_a, home_b, found_output, found_grad, output, token_grad, grad_a, grad_b,
    ha, hb, held, held_b, held_grad, held_output, in_sems, out_sems,
):
    rows, owned = token_grad.shape[0], grad_b.shape[0]
    part = home_a.shape[2]
    z = lax.axis_index("grp")
    count = rows // 4
    bands = [pl.ds(k * count, count) for k in range(4)]
    moves = [(home_a, ha, None), (home_b, hb, None)]
    moves += [(found_grad.at[band], held_grad.at[band], token_grad.at[band]) for band in bands]
    moves.append((found_output, held_output, output))
    loads = [pltpu.make_async_copy(move[0], move[1], in_sems.at[k]) for k, move in enumerate(moves)]
    for load in loads:
        load.start()
    stores = []

    def store(source, target):
        stores.append(pltpu.make_async_copy(source, target, out_sems.at[len(stores)]))
        stores[-1].start()

    row = lax.broadcasted_iota(jnp.int32, (owned, 64), 1)
    adapter = lax.broadcasted_iota(jnp.int32, (owned, 64), 0)
    ids = wanted(slot_table, z, owned, row)
    loads[0].wait()
    for i in range(8):
        cols = pl.ds(i * part, part)
        held[:, cols] = mm(pick(ids, row, adapter, i), ha[...].reshape(64, part)).astype(BF16)
        store(held.at[:, cols], grad_a.at[:, cols])
        if i == 1:
            for load, (_, source, target) in zip(loads[2:], moves[2:]):
                load.wait()
                store(source, target)
    loads[1].wait()
    rows_b = hb[...].reshape(64, hb.shape[2])
    line = lax.broadcasted_iota(jnp.int32, rows_b.shape, 0)
    piece = (line % 2) * 4 + (line // 4) % 4
    spread = jnp.concatenate([jnp.where(piece == i, rows_b, 0.0) for i in range(8)], axis=1)
    hits = jnp.where(ids == adapter, 1.0, 0.0).astype(BF16)
    held_b[...] = mm(hits, spread.astype(BF16)).astype(BF16)
    store(held_b, grad_b)
    for copy in stores:
        copy.wait()


def local(tokens, tenant, slot_table, weight, adapter_a, adapter_b, cotangent):
    rows, width = tokens.shape
    out_width = weight.shape[1]
    owned = adapter_a.shape[0]
    part, part_b = width // 4, out_width // 4
    vmem, hbm = pl.BlockSpec(memory_space=pltpu.VMEM), pl.BlockSpec(memory_space=pltpu.HBM)
    smem = pl.BlockSpec(memory_space=pltpu.SMEM)
    buffer = lambda *shape, dtype=BF16: pltpu.VMEM(shape, dtype)
    found_output, found_grad, home_a, home_b = pl.pallas_call(
        kernel,
        name="exchange_and_multiply",
        out_shape=(
            jax.ShapeDtypeStruct((rows, out_width), BF16),
            jax.ShapeDtypeStruct((rows, width), BF16),
            jax.ShapeDtypeStruct((4, 16, part), BF16),
            jax.ShapeDtypeStruct((4, 16, part_b), BF16),
        ),
        in_specs=[smem, vmem, hbm, hbm, hbm, hbm, hbm],
        out_specs=(hbm, hbm, hbm, hbm),
        scratch_shapes=[
            buffer(2, 4, 4, 2, 128, out_width),
            buffer(2, 4, 4, 16, width),
            buffer(2, 4, 4, 16, out_width),
            buffer(2, rows, width),
            buffer(2, rows, out_width),
            buffer(rows, width),
            buffer(owned, 2 * out_width),
            buffer(4, 4, 16, width),
            buffer(4, 4, 16, out_width),
            buffer(2, 6, 4, 16, part // 2),
            buffer(2, 6, 16, part // 2),
            buffer(2, 6, 4, 16, part // 2),
            buffer(2, 6, 16, part // 2),
            buffer(2, 6, 4, 16, part_b),
            buffer(2, 6, 16, part_b),
            buffer(16, width),
            buffer(16, out_width),
            buffer(rows, 512, dtype=F32),
            buffer(rows, 512, dtype=F32),
            buffer(rows, 512),
            buffer(rows, 512),
            buffer(2, 256, rows),
            buffer(2, 256, rows),
            buffer(256, rows),
            buffer(256, rows),
            buffer(rows, out_width, dtype=F32),
            buffer(rows, out_width),
            buffer(4, 16, part),
            buffer(4, 16, part_b),
            buffer(4, 16, part),
            buffer(4, 16, part_b),
            buffer(4, 16, part),
            buffer(4, 16, part_b),
            buffer(4, 16, part),
            buffer(4, 16, part_b),
            pltpu.SemaphoreType.DMA((11,)),
            pltpu.SemaphoreType.DMA((SENDS,)),
            pltpu.SemaphoreType.DMA((RECEIVES,)),
        ],
        compiler_params=pltpu.CompilerParams(
            collective_id=0, has_side_effects=True, vmem_limit_bytes=62 * 1024 * 1024
        ),
    )(slot_table, tenant.reshape(1, rows), tokens, weight, adapter_a, adapter_b, cotangent)

    return pl.pallas_call(
        place_kernel,
        name="place_results",
        out_shape=(
            jax.ShapeDtypeStruct((rows, out_width), BF16),
            jax.ShapeDtypeStruct((rows, width), BF16),
            jax.ShapeDtypeStruct(adapter_a.shape, BF16),
            jax.ShapeDtypeStruct(adapter_b.shape, BF16),
        ),
        in_specs=[smem, hbm, hbm, hbm, hbm],
        out_specs=(hbm, hbm, hbm, hbm),
        scratch_shapes=[
            buffer(4, 16, part),
            buffer(4, 16, part_b),
            buffer(owned, 2 * width),
            buffer(owned, 2 * out_width),
            buffer(rows, width),
            buffer(rows, out_width),
            pltpu.SemaphoreType.DMA((7,)),
            pltpu.SemaphoreType.DMA((14,)),
        ],
        compiler_params=pltpu.CompilerParams(vmem_limit_bytes=62 * 1024 * 1024),
    )(slot_table, home_a, home_b, found_output, found_grad)


def solution(mesh):
    return jax.shard_map(
        local,
        mesh=mesh,
        in_specs=(
            P(("grp", "fsdp"), None),
            P(("grp", "fsdp")),
            P(),
            P("fsdp", None),
            P("grp", "fsdp"),
            P("grp", "fsdp"),
            P(("grp", "fsdp"), None),
        ),
        out_specs=(
            P(("grp", "fsdp"), None),
            P(("grp", "fsdp"), None),
            P("grp", "fsdp"),
            P("grp", "fsdp"),
        ),
        check_vma=False,
    )
```

```python
import math

import jax
import jax.numpy as jnp
from jax import lax
from jax.experimental import pallas as pl
from jax.experimental.pallas import tpu as pltpu
from jax.sharding import PartitionSpec as P

SCALE = 2.0
RING = 4
SENDS = 40
RECEIVES = 92
ORDER = (
    "w.s1", "swapb", "swapa", "d.s1", "b.s1", "tokx", "mask", "w.s2", "d.s2", "a.s1", "b.s2", "w.s3", "z0.go",
    "z1.go", "b.s3", "a.s2", "d.s3", "z0.fw", "b.s4", "a.s3", "w.s4", "z2.go", "z0.en", "b.s5", "z3.go",
    "d.s4", "z1.fw", "z2.fw", "z4.go", "b.fin", "back", "T0", "a.s4", "T1", "T2", "d.s5", "z5.go", "T3",
    "z1.en", "r1.s1", "r0.s1", "w.s5", "d.fin", "z2.en", "o1.0", "o2.0", "z3.fw", "o0.0", "o1.1", "z4.fw",
    "a.s5", "o0.1", "a.fin", "z6.go", "low0", "low1", "r1.s2", "z3.en", "x0.0", "x1.0", "z4.en", "z5.fw",
    "tb", "q.s1", "x2.0", "o4.0", "o3.0", "z7.go", "r0.s2", "x3.0", "x0.1", "x4.0", "x3.1", "q.s2", "r1.s3",
    "z5.en", "o2.1", "o3.1", "x1.1", "z6.fw", "x2.1", "r0.s3", "o5.0", "q.s3", "x4.1", "r1.s4", "tot",
    "z7.fw", "x5.0", "r0.s4", "x5.1", "z6.en", "q.s4", "o4.1", "o5.1", "r1.s5", "hom1", "o6.0", "x6.0",
    "r0.s5", "hom0", "z7.en", "q.s5", "o6.1", "homb", "x6.1", "o7.0", "x7.0", "o7.1", "x7.1", "homw", "out",
)
SHARED = 16
OFFSETS = (0, -1, 1, 2)
MESH = pl.DeviceIdType.MESH
ALL = slice(None)
BF16 = jnp.bfloat16
F32 = jnp.float32


def mod(value):
    return lax.rem(value + RING, RING)


def mm(left, right):
    return jnp.dot(left, right, preferred_element_type=F32)


def mm_last(left, right):
    return lax.dot_general(left, right, (((1,), (1,)), ((), ())), preferred_element_type=F32)


def mm_first(left, right):
    return lax.dot_general(left, right, (((0,), (0,)), ((), ())), preferred_element_type=F32)


class Net:
    def __init__(self, send_sems, recv_sems):
        self.z = lax.axis_index("grp")
        part = lax.axis_index("fsdp")
        self.c = lax.rem(part, 2)
        self.y = lax.rem(part // 2, RING)
        self.x = part // (2 * RING)
        self.send_sems, self.recv_sems, self.started, self.places = send_sems, recv_sems, [], 0

    def at(self, dx=0, dy=0, dz=0, dc=0):
        x, y, z = mod(self.x + dx), mod(self.y + dy), mod(self.z + dz)
        c = lax.rem(self.c + dc, 2)
        return (z, (x * RING + y) * 2 + c)

    def plane(self, axis, step):
        return self.at(dx=step) if axis == 0 else self.at(dy=step)

    def place(self):
        self.places += 1
        return self.recv_sems.at[self.places - 1]

    def send(self, source, target, device, sem=None):
        k = len(self.started)
        if k >= SENDS:
            self.started[k - SENDS].wait_send()
        copy = pltpu.make_async_remote_copy(
            src_ref=source,
            dst_ref=target,
            send_sem=self.send_sems.at[k % SENDS],
            recv_sem=self.place() if sem is None else sem,
            device_id=device,
            device_id_type=MESH,
        )
        copy.start()
        self.started.append(copy)
        return copy

    def sibling(self, ref, sem=None):
        return self.send(ref, ref, self.at(dc=1), sem)


def wait_all(region, sem):
    pltpu.make_async_copy(region, region, sem).wait()


class Gather:
    def __init__(self, net, ref, cut, to_sibling=True):
        self.net, self.buffer, self.cut = net, ref, cut
        self.near, self.far, self.line, self.rest = [[net.place(), net.place()] for _ in range(4)]
        self.passed = net.place() if to_sibling else None

    def ref(self, half, p, s, part, count):
        x, y = (p, s) if half == 0 else (s, p)
        return self.buffer.at[(self.net.c, x, y) + self.cut(half, part, count)]

    def at(self, half):
        return (self.net.x, self.net.y) if half == 0 else (self.net.y, self.net.x)

    def move(self, ref, axis, step, sem=None):
        return self.net.send(ref, ref, self.net.plane(axis, step), sem)

    def hand(self, ref):
        if self.passed is not None:
            self.net.sibling(ref, self.passed)

    def s1(self):
        for half in (0, 1):
            p, s = self.at(half)
            own = self.ref(half, p, s, 0, 2)
            self.move(own, half, 1, self.near[half])
            self.move(own, half, -1, self.near[half])

    def s2(self):
        for half in (0, 1):
            p, s = self.at(half)
            wait_all(self.ref(half, pl.ds(0, 2), s, 0, 2), self.near[half])
            self.move(self.ref(half, mod(p - 1), s, 0, 1), half, 1, self.far[half])
            self.move(self.ref(half, mod(p + 1), s, 1, 1), half, -1, self.far[half])

    def s3(self):
        for half in (0, 1):
            p, s = self.at(half)
            wait_all(self.ref(half, mod(p + 2), s, 0, 2), self.far[half])
            own = self.ref(half, ALL, s, 0, 2)
            self.move(own, 1 - half, 1, self.line[half])
            self.move(own, 1 - half, -1, self.line[half])
            self.hand(own)

    def s4(self):
        for half in (0, 1):
            _, s = self.at(half)
            wait_all(self.ref(half, ALL, pl.ds(0, 2), 0, 2), self.line[half])
            self.move(self.ref(half, ALL, mod(s - 1), 0, 1), 1 - half, 1, self.rest[half])
            self.move(self.ref(half, ALL, mod(s + 1), 1, 1), 1 - half, -1, self.rest[half])
            self.hand(self.ref(half, ALL, mod(s - 1), 0, 2))
            self.hand(self.ref(half, ALL, mod(s + 1), 0, 2))

    def s5(self):
        for half in (0, 1):
            _, s = self.at(half)
            last = self.ref(half, ALL, mod(s + 2), 0, 2)
            wait_all(last, self.rest[half])
            self.hand(last)

    def fin(self):
        wait_all(self.buffer.at[(1 - self.net.c, ALL, ALL) + self.cut(None, 0, 2)], self.passed)


class Scatter:
    def __init__(self, net, terms, line_slots, block_slots, out, cols):
        self.net, self.terms, self.out, self.cols = net, terms, out, cols
        self.line_slots, self.block_slots = line_slots, block_slots
        self.sems = [[[net.place(), net.place()] for _ in range(2)] for _ in range(2)]

    def index(self, half, p, s, part):
        x, y = (p, s) if half == 0 else (s, p)
        return x, y, ALL, self.cols(half, part)

    def at(self, half):
        return (self.net.x, self.net.y) if half == 0 else (self.net.y, self.net.x)

    def first(self, half, slots, axis, block, sems):
        me = self.net.x if axis == 0 else self.net.y
        ahead, behind = self.net.plane(axis, 1), self.net.plane(axis, -1)
        at, slots, net = self.terms.at, slots.at, self.net
        net.send(at[block(mod(me + 2), 0)], slots[half, 0], ahead, sems[0])
        net.send(at[block(mod(me + 2), 1)], slots[half, 1], behind, sems[0])
        net.send(at[block(mod(me + 1), 1)], slots[half, 2], ahead, sems[1])
        net.send(at[block(mod(me - 1), 0)], slots[half, 3], behind, sems[1])

    def add(self, block, slots):
        total = self.terms[block].astype(F32)
        for slot in slots:
            total = total + slot.astype(F32)
        return total

    def s1(self):
        for half in (0, 1):
            self.first(
                half,
                self.line_slots,
                half,
                lambda p, part, h=half: self.index(h, p, ALL, part),
                self.sems[0][half],
            )

    def s2(self):
        for half in (0, 1):
            p, _ = self.at(half)
            sems = self.sems[0][half]
            wait_all(self.line_slots.at[half, pl.ds(0, 2)], sems[0])
            for k, step in ((0, 1), (1, -1)):
                target = mod(p + step)

                def line(i, _, half=half, k=k, target=target):
                    block = self.index(half, target, i, k)
                    self.terms[block] = self.add(block, [self.line_slots[half, k, i]]).astype(BF16)
                    return 0

                lax.fori_loop(0, RING, line, 0)
                self.net.send(
                    self.terms.at[self.index(half, target, ALL, k)],
                    self.line_slots.at[half, 4 + k],
                    self.net.plane(half, step),
                    sems[1],
                )

    def s3(self):
        for half in (0, 1):
            p, _ = self.at(half)
            wait_all(self.line_slots.at[half, pl.ds(2, 4)], self.sems[0][half][1])
            for part in (0, 1):

                def line(i, _, half=half, part=part, p=p):
                    block = self.index(half, p, i, part)
                    slots = [self.line_slots[half, 4 + part, i], self.line_slots[half, 3 - part, i]]
                    self.terms[block] = self.add(block, slots).astype(BF16)
                    return 0

                lax.fori_loop(0, RING, line, 0)
            self.first(
                half,
                self.block_slots,
                1 - half,
                lambda s, part, h=half, p=p: self.index(h, p, s, part),
                self.sems[1][half],
            )

    def s4(self):
        for half in (0, 1):
            p, s = self.at(half)
            sems = self.sems[1][half]
            wait_all(self.block_slots.at[half, pl.ds(0, 2)], sems[0])
            for k, step in ((0, 1), (1, -1)):
                block = self.index(half, p, mod(s + step), k)
                self.terms[block] = self.add(block, [self.block_slots[half, k]]).astype(BF16)
                self.net.send(
                    self.terms.at[block],
                    self.block_slots.at[half, 4 + k],
                    self.net.plane(1 - half, step),
                    sems[1],
                )

    def s5(self):
        for half in (0, 1):
            p, s = self.at(half)
            wait_all(self.block_slots.at[half, pl.ds(2, 4)], self.sems[1][half][1])
            for part in (0, 1):
                block = self.index(half, p, s, part)
                slots = [self.block_slots[half, 4 + part], self.block_slots[half, 3 - part]]
                self.out[:, self.cols(half, part)] = self.add(block, slots).astype(BF16)


def swap(net, source, landed):
    sem = net.place()
    for step in (1, 3, 2):
        net.send(source.at[mod(net.z + step)], landed.at[net.z], net.at(dz=step), sem)
    landed[net.z] = source[net.z]
    return landed.at[pl.ds(0, 3)], sem


def fold(q, shape, row_dim):
    row = lax.broadcasted_iota(jnp.int32, shape, row_dim)
    col = lax.broadcasted_iota(jnp.int32, shape, 1 - row_dim)
    same = (row // 4 == col // 16) & (row % 4 == col % 4) & ((col // 4) % 4 == q)
    return jnp.where(same, 1.0, 0.0).astype(BF16)


def wanted(slot_table, z, owned, row):
    found = jnp.zeros(row.shape, jnp.int32)
    for g in range(4):
        for j in range(2):
            here = (row // 16 == g) & ((row // 2) % 2 == j)
            found = found + jnp.where(here, slot_table[g, 2 * z + j] - z * owned, 0)
    return found


def pick(ids, row, adapter, i):
    here = (ids == adapter) & ((row % 2) * 4 + (row // 4) % 4 == i)
    return jnp.where(here, 1.0, 0.0).astype(BF16)


def kernel(
    slot_table, tenant, tokens, weight, adapter_a, adapter_b, cotangent,
    output, token_grad, home_a, home_b,
    w, sa, sb, tok, cot, tg, ab, t_a, t_b, lx_0, ly_0, lx_1, ly_1, lx_b, ly_b, g_a, g_b,
    mask, partial, back, low, back_t, low_t, back_x, low_x, total, held, pa, pb, ma, mb, ha, hb, na, nb,
    local_sems, send_sems, recv_sems,
):
    net = Net(send_sems, recv_sems)
    x, y, z, c = net.x, net.y, net.z, net.c
    width, out_width = tokens.shape[1], weight.shape[1]
    rows = tokens.shape[0]
    owned = adapter_a.shape[0]
    part_a, part_b = width // 4, out_width // 4
    row_scale = 1.0 / math.sqrt(rows * 2 * RING * RING)
    shared, rest, quarter = pl.ds(0, SHARED), pl.ds(SHARED, 128 - SHARED), out_width // 4

    def slab_cols(dz, part=0, count=2):
        start = mod(z + dz) * quarter + part * (quarter // 2)
        return pl.ds(pl.multiple_of(start, quarter // 2), count * (quarter // 2))

    loads = []

    def load(source, target):
        loads.append(pltpu.make_async_copy(source, target, local_sems.at[len(loads)]))
        loads[-1].start()

    for h in (0, 1):
        load(weight.at[pl.ds(h * 128 + SHARED, 128 - SHARED)], w.at[c, x, y, h, rest])
    for h in (0, 1):
        load(weight.at[pl.ds(h * 128, SHARED)], w.at[c, x, y, h, shared])
    load(adapter_b, ab)
    for r in (0, 1):
        load(adapter_a.at[:, pl.ds(r * width, width)], tg.at[pl.ds(r * 128, 128)])
    load(cotangent, cot.at[c])
    load(tokens, tok.at[c])

    barrier = pltpu.get_barrier_semaphore()
    partners = [net.at(dx=1), net.at(dx=-1), net.at(dy=1), net.at(dy=-1), net.at(dz=1), net.at(dz=-1)]
    partners += [net.at(dz=2), net.at(dc=1)]
    for device in partners:
        pl.semaphore_signal(barrier, inc=1, device_id=device, device_id_type=MESH)

    steps, state = {}, {}

    def step(name):
        def keep(function):
            steps[name] = function
            return function

        return keep

    def stages(name, collective):
        for stage in ("s1", "s2", "s3", "s4", "s5", "fin"):
            if hasattr(collective, stage):
                steps[name + "." + stage] = getattr(collective, stage)

    def cut_cols(width):
        def cut(half, part, count):
            return ALL, ALL if half is None else pl.ds((half * 2 + part) * (width // 4), count * (width // 4))

        return cut

    def cut_slab(half, part, count):
        return half, rest, slab_cols(0, part, count)

    def cut_shared(half, part, count):
        return ALL if half is None else half, shared, pl.ds(part * (out_width // 2), count * (out_width // 2))

    gather_w = Gather(net, w, cut_slab, to_sibling=False)
    gather_d = Gather(net, w, cut_shared)
    gather_a = Gather(net, sa, cut_cols(width))
    gather_b = Gather(net, sb, cut_cols(out_width))
    stages("w", gather_w)
    stages("d", gather_d)
    stages("a", gather_a)
    stages("b", gather_b)

    def wave(v):
        return lambda half, part: pl.ds((half * 2 + part) * part_a + v * (part_a // 2), part_a // 2)

    stages("r0", Scatter(net, t_a, lx_0, ly_0, g_a, wave(0)))
    stages("r1", Scatter(net, t_a, lx_1, ly_1, g_a, wave(1)))
    stages("q", Scatter(net, t_b, lx_b, ly_b, g_b, lambda half, part: pl.ds((half * 2 + part) * part_b, part_b)))

    @step("w.s1")
    def _():
        loads[0].wait()
        loads[1].wait()
        gather_w.s1()

    @step("d.s1")
    def _():
        loads[2].wait()
        loads[3].wait()
        gather_d.s1()

    def all_picks():
        row = lax.broadcasted_iota(jnp.int32, (64, owned), 0)
        adapter = lax.broadcasted_iota(jnp.int32, (64, owned), 1)
        ids = wanted(slot_table, z, owned, row)
        return [pick(ids, row, adapter, i) for i in range(8)]

    @step("mask")
    def _():
        slot = lax.broadcasted_iota(jnp.int32, (16, rows), 0) // 2
        slot_ids = jnp.zeros((16, rows), jnp.int32)
        for s in range(8):
            slot_ids = slot_ids + jnp.where(slot == s, slot_table[z, s], 0)
        hit = jnp.where(slot_ids == tenant[...], 1.0, 0.0)
        mask[...] = jnp.concatenate([hit] * 32, axis=0).T
        total[...] = jnp.zeros_like(total)

    @step("swapb")
    def _():
        loads[4].wait()
        picks = state["picks"] = all_picks()
        chosen = jnp.zeros((64, part_b), F32)
        for i in range(8):
            chosen += mm(picks[i], ab[:, i * part_b : (i + 1) * part_b])
        pb[...] = chosen.astype(BF16).reshape(pb.shape)
        state["lb"] = swap(net, pb, mb)

    @step("swapa")
    def _():
        loads[5].wait()
        loads[6].wait()
        picks = state["picks"]

        def pick_a(k, _):
            cols = pl.ds(pl.multiple_of(k * 512, 512), 512)
            chosen = jnp.zeros((64, 512), F32)
            for i in range(8):
                r, q = i // 4, i % 4
                from_cols = pl.ds(pl.multiple_of(q * part_a + k * 512, 512), 512)
                chosen += mm(picks[i], tg[r * 128 : (r + 1) * 128, from_cols])
            pa[:, :, cols] = chosen.astype(BF16).reshape(4, 16, 512)
            return 0

        lax.fori_loop(0, part_a // 512, pick_a, 0)
        state["la"] = swap(net, pa, ma)

    @step("tokx")
    def _():
        loads[7].wait()
        loads[8].wait()
        state["cx"] = net.sibling(cot.at[c])
        state["tx"] = net.sibling(tok.at[c])

    @step("b.s1")
    def _():
        wait_all(*state["lb"])
        landed = mb[...].reshape(64, part_b)
        for q in range(4):
            sb[c, x, y, :, q * part_b : (q + 1) * part_b] = mm(fold(q, (16, 64), 0), landed).astype(BF16)
        gather_b.s1()

    @step("a.s1")
    def _():
        wait_all(*state["la"])
        landed = ma[...].reshape(64, part_a)
        for q in range(4):
            sa[c, x, y, :, q * part_a : (q + 1) * part_a] = mm(fold(q, (16, 64), 0), landed).astype(BF16)
        gather_a.s1()

    ring, ring_far, passed, stored = {}, {}, {}, []

    def place_of(n, i):
        offset, h = OFFSETS[n // 2], n % 2
        return (i, mod(y + offset)) if h == 0 else (mod(x + offset), i)

    def line_of(n, cols):
        count = 3 if n < 2 else 4
        return w.at[(c,) + place_of(n, pl.ds(0, count)) + (n % 2, rest, cols)]

    def slabs_of(n, cols):
        if n >= 2:
            return [line_of(n, cols)]
        others = [mod((x if n == 0 else y) + k) for k in (1, 2, 3)]
        return [w.at[(c,) + place_of(n, i) + (n % 2, rest, cols)] for i in others]

    def z_start(n):
        ring[n], ring_far[n], passed[n] = net.place(), net.place(), net.place()
        for own in slabs_of(n, slab_cols(0)):
            net.send(own, own, net.at(dz=1), ring[n])
            net.send(own, own, net.at(dz=-1), ring[n])
            net.sibling(own, passed[n])
        if n < 2:
            net.sibling(w.at[c, x, y, n % 2, rest], passed[n])

    def z_forward(n):
        wait_all(line_of(n, pl.ds(0, 2 * quarter)), ring[n])
        for one in slabs_of(n, slab_cols(-1, 0, 1)):
            net.send(one, one, net.at(dz=1), ring_far[n])
        for two in slabs_of(n, slab_cols(1, 1, 1)):
            net.send(two, two, net.at(dz=-1), ring_far[n])
        for slab in slabs_of(n, slab_cols(-1)) + slabs_of(n, slab_cols(1)):
            net.sibling(slab, passed[n])

    def z_end(n):
        wait_all(line_of(n, slab_cols(2)), ring_far[n])
        for last in slabs_of(n, slab_cols(2)):
            net.sibling(last, passed[n])

    def blocks_of(n, i):
        h, cols, blocks = n % 2, [], []
        for px, py in (place_of(n, 2 * i), place_of(n, 2 * i + 1)):
            for core in (0, 1):
                start = ((px * RING + py) * 2 + core) * 256 + h * 128
                cols.append(pl.ds(pl.multiple_of(start, 128), 128))
                blocks.append(w[core, px, py, h])
        return cols, jnp.concatenate(blocks, axis=0)

    def multiply_out(n, i):
        if i == 0:
            wait_all(w.at[(1 - c,) + place_of(n, ALL) + (n % 2, rest)], passed[n])
        cols, block = blocks_of(n, i)
        total[...] += mm(jnp.concatenate([tok[c, :, at] for at in cols], axis=1), block)

    def multiply_back(n, i):
        cols, block = blocks_of(n, i)
        from_a = mm(back[...], jnp.concatenate([sa[:, :, :, :, at].reshape(512, 128) for at in cols], axis=1))
        found = (mm_last(cot[c], block) + from_a).astype(BF16)
        for k, at in enumerate(cols):
            tg[:, at] = found[:, k * 128 : (k + 1) * 128]
            pltpu.make_async_copy(tg.at[:, at], token_grad.at[:, at], local_sems.at[n]).start()

    for n in range(8):
        steps["z%d.go" % n] = lambda n=n: z_start(n)
        steps["z%d.fw" % n] = lambda n=n: z_forward(n)
        steps["z%d.en" % n] = lambda n=n: z_end(n)
        for i in range(2):
            steps["o%d.%d" % (n, i)] = lambda n=n, i=i: multiply_out(n, i)
            steps["x%d.%d" % (n, i)] = lambda n=n, i=i: multiply_back(n, i)

    stack_b = lambda: sb[...].reshape(512, out_width)

    @step("back")
    def _():
        found = SCALE * mask[...] * mm_last(cot[c], stack_b())
        back[...] = found.astype(BF16)
        back_t[...] = found.T.astype(BF16).reshape(2, 256, rows)
        state["bx"] = net.send(back_t.at[1 - c], back_x, net.at(dc=1))

    def terms_a(i):
        if i == 0:
            state["tx"].wait_recv()
            state["cx"].wait_recv()
            state["bx"].wait_recv()

        def chunk(k, _):
            start = (k // 2) * part_a + (i // 2) * (part_a // 2) + (k % 2) * 512
            cols = pl.ds(pl.multiple_of(start, 512), 512)
            found = mm(back_t[c], tok[c, :, cols]) + mm(back_x[...], tok[1 - c, :, cols])
            t_a[:, :, :, cols] = (found * row_scale).astype(BF16).reshape(4, 4, 16, 512)
            return 0

        count = width // 2048
        lax.fori_loop(i % 2 * count, (i % 2 + 1) * count, chunk, 0)

    for i in range(4):
        steps["T%d" % i] = lambda i=i: terms_a(i)

    def low_sum(i):
        cols = pl.ds(i * (width // 2), width // 2)
        return mm_last(tok[c, :, cols], sa[:, :, :, :, cols].reshape(512, width // 2))

    @step("low0")
    def _():
        partial[...] = low_sum(0)

    @step("low1")
    def _():
        found = mask[...] * (partial[...] + low_sum(1))
        low[...] = found.astype(BF16)
        low_t[...] = found.T.astype(BF16).reshape(2, 256, rows)
        state["lx"] = net.send(low_t.at[1 - c], low_x, net.at(dc=1))

    @step("tot")
    def _():
        total[...] += SCALE * mm(low[...], stack_b())

    @step("tb")
    def _():
        state["lx"].wait_recv()
        found = mm(low_t[c], cot[c]) + mm(low_x[...], cot[1 - c])
        t_b[...] = (found * (SCALE * row_scale)).astype(BF16).reshape(4, 4, 16, out_width)

    def unfold(source, size, start, count):
        found = jnp.zeros((64, count), F32)
        for q in range(4):
            found += mm(fold(q, (64, 16), 1), source[:, q * size + start : q * size + start + count])
        return found.astype(BF16).reshape(4, 16, count)

    def go_home(v):
        cols = pl.ds(v * (part_a // 2), part_a // 2)
        na[:, :, cols] = unfold(g_a, part_a, v * (part_a // 2), part_a // 2)
        state["ha%d" % v] = swap(net, na.at[:, :, cols], ha.at[:, :, cols])

    steps["hom0"] = lambda: go_home(0)
    steps["hom1"] = lambda: go_home(1)

    def store(source, target, k):
        stored.append(pltpu.make_async_copy(source, target, local_sems.at[k]))
        stored[-1].start()

    @step("homb")
    def _():
        nb[...] = unfold(g_b, part_b, 0, part_b)
        state["hb"] = swap(net, nb, hb)

    @step("homw")
    def _():
        wait_all(*state["ha0"])
        wait_all(*state["ha1"])
        wait_all(*state["hb"])
        store(ha, home_a, 8)
        store(hb, home_b, 9)

    @step("out")
    def _():
        held[...] = total[...].astype(BF16)
        store(held, output, 10)

    pl.semaphore_wait(barrier, len(partners))
    for name in ORDER:
        steps[name]()
    for copy in stored:
        copy.wait()
    for n in range(8):
        wait_all(tg.at[:, pl.ds(0, 1024)], local_sems.at[n])
    for copy in net.started[-SENDS:]:
        copy.wait_send()


def place_kernel(
    slot_table, home_a, home_b, found_output, found_grad, output, token_grad, grad_a, grad_b,
    ha, hb, held, held_b, held_grad, held_output, in_sems, out_sems,
):
    rows, owned = token_grad.shape[0], grad_b.shape[0]
    part = home_a.shape[2]
    z = lax.axis_index("grp")
    count = rows // 4
    bands = [pl.ds(k * count, count) for k in range(4)]
    moves = [(home_a, ha, None), (home_b, hb, None)]
    moves += [(found_grad.at[band], held_grad.at[band], token_grad.at[band]) for band in bands]
    moves.append((found_output, held_output, output))
    loads = [pltpu.make_async_copy(move[0], move[1], in_sems.at[k]) for k, move in enumerate(moves)]
    for load in loads:
        load.start()
    stores = []

    def store(source, target):
        stores.append(pltpu.make_async_copy(source, target, out_sems.at[len(stores)]))
        stores[-1].start()

    row = lax.broadcasted_iota(jnp.int32, (owned, 64), 1)
    adapter = lax.broadcasted_iota(jnp.int32, (owned, 64), 0)
    ids = wanted(slot_table, z, owned, row)
    loads[0].wait()
    for i in range(8):
        cols = pl.ds(i * part, part)
        held[:, cols] = mm(pick(ids, row, adapter, i), ha[...].reshape(64, part)).astype(BF16)
        store(held.at[:, cols], grad_a.at[:, cols])
        if i == 1:
            for load, (_, source, target) in zip(loads[2:], moves[2:]):
                load.wait()
                store(source, target)
    loads[1].wait()
    rows_b = hb[...].reshape(64, hb.shape[2])
    line = lax.broadcasted_iota(jnp.int32, rows_b.shape, 0)
    piece = (line % 2) * 4 + (line // 4) % 4
    spread = jnp.concatenate([jnp.where(piece == i, rows_b, 0.0) for i in range(8)], axis=1)
    hits = jnp.where(ids == adapter, 1.0, 0.0).astype(BF16)
    held_b[...] = mm(hits, spread.astype(BF16)).astype(BF16)
    store(held_b, grad_b)
    for copy in stores:
        copy.wait()


def local(tokens, tenant, slot_table, weight, adapter_a, adapter_b, cotangent):
    rows, width = tokens.shape
    out_width = weight.shape[1]
    owned = adapter_a.shape[0]
    part, part_b = width // 4, out_width // 4
    vmem, hbm = pl.BlockSpec(memory_space=pltpu.VMEM), pl.BlockSpec(memory_space=pltpu.HBM)
    smem = pl.BlockSpec(memory_space=pltpu.SMEM)
    buffer = lambda *shape, dtype=BF16: pltpu.VMEM(shape, dtype)
    found_output, found_grad, home_a, home_b = pl.pallas_call(
        kernel,
        name="exchange_and_multiply",
        out_shape=(
            jax.ShapeDtypeStruct((rows, out_width), BF16),
            jax.ShapeDtypeStruct((rows, width), BF16),
            jax.ShapeDtypeStruct((4, 16, part), BF16),
            jax.ShapeDtypeStruct((4, 16, part_b), BF16),
        ),
        in_specs=[smem, vmem, hbm, hbm, hbm, hbm, hbm],
        out_specs=(hbm, hbm, hbm, hbm),
        scratch_shapes=[
            buffer(2, 4, 4, 2, 128, out_width),
            buffer(2, 4, 4, 16, width),
            buffer(2, 4, 4, 16, out_width),
            buffer(2, rows, width),
            buffer(2, rows, out_width),
            buffer(rows, width),
            buffer(owned, 2 * out_width),
            buffer(4, 4, 16, width),
            buffer(4, 4, 16, out_width),
            buffer(2, 6, 4, 16, part // 2),
            buffer(2, 6, 16, part // 2),
            buffer(2, 6, 4, 16, part // 2),
            buffer(2, 6, 16, part // 2),
            buffer(2, 6, 4, 16, part_b),
            buffer(2, 6, 16, part_b),
            buffer(16, width),
            buffer(16, out_width),
            buffer(rows, 512, dtype=F32),
            buffer(rows, 512, dtype=F32),
            buffer(rows, 512),
            buffer(rows, 512),
            buffer(2, 256, rows),
            buffer(2, 256, rows),
            buffer(256, rows),
            buffer(256, rows),
            buffer(rows, out_width, dtype=F32),
            buffer(rows, out_width),
            buffer(4, 16, part),
            buffer(4, 16, part_b),
            buffer(4, 16, part),
            buffer(4, 16, part_b),
            buffer(4, 16, part),
            buffer(4, 16, part_b),
            buffer(4, 16, part),
            buffer(4, 16, part_b),
            pltpu.SemaphoreType.DMA((11,)),
            pltpu.SemaphoreType.DMA((SENDS,)),
            pltpu.SemaphoreType.DMA((RECEIVES,)),
        ],
        compiler_params=pltpu.CompilerParams(
            collective_id=0, has_side_effects=True, vmem_limit_bytes=62 * 1024 * 1024
        ),
    )(slot_table, tenant.reshape(1, rows), tokens, weight, adapter_a, adapter_b, cotangent)

    return pl.pallas_call(
        place_kernel,
        name="place_results",
        out_shape=(
            jax.ShapeDtypeStruct((rows, out_width), BF16),
            jax.ShapeDtypeStruct((rows, width), BF16),
            jax.ShapeDtypeStruct(adapter_a.shape, BF16),
            jax.ShapeDtypeStruct(adapter_b.shape, BF16),
        ),
        in_specs=[smem, hbm, hbm, hbm, hbm],
        out_specs=(hbm, hbm, hbm, hbm),
        scratch_shapes=[
            buffer(4, 16, part),
            buffer(4, 16, part_b),
            buffer(owned, 2 * width),
            buffer(owned, 2 * out_width),
            buffer(rows, width),
            buffer(rows, out_width),
            pltpu.SemaphoreType.DMA((7,)),
            pltpu.SemaphoreType.DMA((14,)),
        ],
        compiler_params=pltpu.CompilerParams(vmem_limit_bytes=62 * 1024 * 1024),
    )(slot_table, home_a, home_b, found_output, found_grad)


def solution(mesh):
    return jax.shard_map(
        local,
        mesh=mesh,
        in_specs=(
            P(("grp", "fsdp"), None),
            P(("grp", "fsdp")),
            P(),
            P("fsdp", None),
            P("grp", "fsdp"),
            P("grp", "fsdp"),
            P(("grp", "fsdp"), None),
        ),
        out_specs=(
            P(("grp", "fsdp"), None),
            P(("grp", "fsdp"), None),
            P("grp", "fsdp"),
            P("grp", "fsdp"),
        ),
        check_vma=False,
    )
```
